512 devices in a mesh: rows: 64 (over z_hi, y, core), feat: 8 (over x, z_lo).
Axes of the slice: x: 4, y: 8, z: 8 (z_hi: 4, z_lo: 2; z = z_hi * 2 + z_lo), core: 2. Of those that a mesh axis runs over, the one named last changes fastest.
Arguments:
- features: bfloat16 [16384, 6144], P('rows', 'feat'), may hold values from -80 to 80
- labels: int32 [16384], P('rows'), may hold values from 0 to 511
- probe_weight: bfloat16 [6144, 512], P('feat'), may hold values from -1 to 1
- sampled: int32 [14336], P('rows'), may hold values from 0 to 255
Outputs:
- newton_step: bfloat16 [6144, 512], P('feat')
- cg_residual: bfloat16 [6144, 512], P('feat')
The draws below stay inside these ranges and needn't reach their ends.
All inputs are finite; a program needn't handle non-finite values.
Results may differ from the reference program's by a relative error of at most 0.023.
Values may be sent and summed in bfloat16 or wider, within the bound.
A program may use at most 64 MiB of HBM per device.

```python
import math
import jax
import jax.numpy as jnp

D = 6144
C = 512
R = 256
S = 224
ROWS_ALL = 16384
SAMPLES = 14336
N_FEAT = 8


def shared_normal(key):
    return jnp.clip(jax.random.normal(key, (D, C), jnp.float32), -6.0, 6.0)


def draw_probe_weight(key, part):
    base = shared_normal(key)
    weight = base * (3.0 / math.sqrt(D))
    return jnp.clip(weight, -1.0, 1.0).astype(jnp.bfloat16)


def draw_features(key, part):
    key = jax.random.fold_in(key, 12)
    first = jax.random.fold_in(key, 0)
    column = jax.lax.broadcasted_iota(jnp.float32, (1, D), 1)
    scales = jnp.exp(math.log(3.0) * column / D)
    values = jnp.clip(jax.random.normal(first, (ROWS_ALL, D), jnp.float32), -6.0, 6.0) * scales
    return jnp.clip(values, -80.0, 80.0).astype(jnp.bfloat16)


def set_ends(result, key, least, top_value):
    longest = result.shape.index(max(result.shape))
    spots = []
    for shift in (0, 1):
        where = [jax.random.randint(jax.random.fold_in(key, axis), (), 0, length) for axis, length in enumerate(result.shape)]
        where[longest] = (where[longest] + shift) % result.shape[longest]
        spots.append(tuple(where))
    return result.at[spots[0]].set(least).at[spots[1]].set(top_value)


def setup_inputs(seed: int = 0) -> dict:
    arg_keys = jax.random.split(jax.random.key(seed), 5)
    features = draw_features(jax.random.fold_in(arg_keys[4], 71), 0)
    labels = set_ends(jax.random.randint(arg_keys[1], (ROWS_ALL,), 0, C), jax.random.fold_in(arg_keys[1], 1), 0, C - 1).astype(jnp.int32)
    probe_weight = draw_probe_weight(jax.random.fold_in(arg_keys[4], 71), 0)
    sampled = set_ends(jax.random.randint(arg_keys[3], (SAMPLES,), 0, R), jax.random.fold_in(arg_keys[3], 1), 0, R - 1).astype(jnp.int32)
    return {"features": features, "labels": labels, "probe_weight": probe_weight, "sampled": sampled}


damping = 0.01


def blocked_product(left, right):
    width = left.shape[1] // N_FEAT
    total = jnp.zeros((left.shape[0], right.shape[1]), jnp.float32)
    for block in range(N_FEAT):
        part = jnp.dot(left[:, block * width:(block + 1) * width], right[block * width:(block + 1) * width], preferred_element_type=jnp.float32)
        total = total + part
    return total


def reference(features, labels, probe_weight, sampled):
    logits = blocked_product(features, probe_weight)
    probs = jax.nn.softmax(logits, axis=-1)
    classes = jnp.arange(C, dtype=jnp.int32)
    onehot = (labels[:, None] == classes[None, :]).astype(jnp.float32)
    err = ((probs - onehot) / ROWS_ALL).astype(jnp.bfloat16)
    grad = jnp.dot(features.T, err, preferred_element_type=jnp.float32) + damping * probe_weight.astype(jnp.float32)
    index = ((jnp.arange(SAMPLES, dtype=jnp.int32) // S) * R + sampled).astype(jnp.int32)
    chosen = features[index]
    chosen_probs = probs[index]
    proj = blocked_product(chosen, grad.astype(jnp.bfloat16))
    inner = jnp.sum(chosen_probs * proj, axis=-1, keepdims=True)
    weighted = ((chosen_probs * proj - chosen_probs * inner) / SAMPLES).astype(jnp.bfloat16)
    image = jnp.dot(chosen.T, weighted, preferred_element_type=jnp.float32) + damping * grad
    norm_sq = jnp.sum(grad * grad)
    curv = jnp.sum(grad * image)
    alpha = norm_sq / curv
    return (-alpha * grad).astype(jnp.bfloat16), (-grad + alpha * image).astype(jnp.bfloat16)
```

```python
import functools

import jax
import jax.numpy as jnp
from jax import lax
from jax.experimental import pallas as pl
from jax.experimental.pallas import tpu as pltpu
from jax.sharding import PartitionSpec as P

MESH = pl.DeviceIdType.MESH
DAMPING = 0.01
F32, BF16 = jnp.float32, jnp.bfloat16
NF, NZ, NY = 8, 4, 8


def kernel(x_ref, lab_ref, w_ref, smp_ref, step_ref, res_ref, xt, part, got_l, err, probs, g_keep, g_out, g_in, g_sum,
           g_ya, g_zb, g_a2, g_b2, g_za, g_yb, grad_a, grad_b, grad, proj, got_p, wgt, i_keep, i_out, i_in, i_sum,
           i_ya, i_zb, i_a2, i_b2, i_za, i_yb, resid, sc_f, sc_c, sc_y, sc_z, sends, recvs):
    rows = lax.axis_index("rows")
    feat = lax.axis_index("feat")
    core = lax.rem(rows, 2)
    y = lax.rem(rows // 2, NY)
    z = rows // (2 * NY)
    height = x_ref.shape[0]
    own = height // NF
    half = w_ref.shape[1] // 2
    total_rows = height * NF * 8
    total_samples = smp_ref.shape[1] * NF * 8

    def to_feat(k):
        return {"rows": rows, "feat": lax.rem(feat + k, NF)}

    def to_y(k):
        return {"rows": (z * NY + lax.rem(y + k, NY)) * 2 + core, "feat": feat}

    def to_z(k):
        return {"rows": (lax.rem(z + k, NZ) * NY + y) * 2 + core, "feat": feat}

    partner = {"rows": rows + 1 - 2 * core, "feat": feat}
    order_8 = (4, 3, 5, 2, 6, 1, 7)
    order_4 = (2, 1, 3)

    pending = []

    def send(src, dst, where):
        index = len(pending)
        copy = pltpu.make_async_remote_copy(
            src_ref=src, dst_ref=dst, send_sem=sends.at[index], recv_sem=recvs.at[index], device_id=where,
            device_id_type=MESH,
        )
        copy.start()
        pending.append(copy)
        return copy

    def arrive(copies):
        for copy in copies:
            copy.wait_recv()

    barrier = pltpu.get_barrier_semaphore()
    peers = [partner] + [to_feat(k) for k in order_8] + [to_y(k) for k in order_8] + [to_z(k) for k in order_4]
    for where in peers:
        pl.semaphore_signal(barrier, inc=1, device_id=where, device_id_type=MESH)

    part[...] = jnp.dot(x_ref[...], w_ref[...], preferred_element_type=F32).reshape(part.shape)
    pl.semaphore_wait(barrier, len(peers))
    copies = [send(part.at[lax.rem(feat + k, NF)], got_l.at[feat], to_feat(k)) for k in order_8]
    xt[...] = x_ref[...].T
    row_id = feat * own + lax.broadcasted_iota(jnp.int32, (own, height), 0)
    here = row_id == lax.broadcasted_iota(jnp.int32, (own, height), 1)
    label = jnp.sum(jnp.where(here, lab_ref[...], 0), axis=1, keepdims=True)
    sample_id = feat * own + lax.broadcasted_iota(jnp.int32, (own, smp_ref.shape[1]), 0)
    count = jnp.sum(jnp.where(sample_id == smp_ref[...], 1.0, 0.0), axis=1, keepdims=True)
    got_l[feat] = part[feat]
    arrive(copies)
    logits = got_l[0]
    for k in range(1, NF):
        logits = logits + got_l[k]
    expo = jnp.exp(logits - jnp.max(logits, axis=1, keepdims=True))
    p = expo / jnp.sum(expo, axis=1, keepdims=True)
    probs[...] = p
    onehot = jnp.where(label == lax.broadcasted_iota(jnp.int32, p.shape, 1), 1.0, 0.0)
    e = ((p - onehot) / total_rows).astype(BF16)
    err[0, feat] = e[:, :half]
    err[1, feat] = e[:, half:]
    arrive([send(err.at[:, feat], err.at[:, feat], to_feat(k)) for k in order_8])

    def reduce_rows(mat, keep, out, into, total, ya, zb, a2, b2, za, yb, ride):
        depth = total.shape[0]
        cut = depth * 2 // 3
        out[...] = jnp.dot(xt[...], mat[1 - core].reshape(height, half), preferred_element_type=F32).astype(BF16)
        copies = [send(out, into, partner)]
        extra = ride(0, copies)
        keep[...] = jnp.dot(xt[...], mat[core].reshape(height, half), preferred_element_type=F32)
        arrive(copies)
        total[...] = (keep[...] + into[...].astype(F32)).astype(BF16)
        copies = []
        for k in order_8:
            there = pl.multiple_of(lax.rem(y + k, NY) * 64, 64)
            copies.append(send(total.at[pl.ds(there, 64)], ya.at[y], to_y(k)))
            if k in order_4:
                there = pl.multiple_of(cut + lax.rem(z + k, NZ) * 64, 64)
                copies.append(send(total.at[pl.ds(there, 64)], zb.at[z], to_z(k)))
        ride(1, copies)
        ya[y] = total[pl.ds(pl.multiple_of(y * 64, 64), 64)]
        zb[z] = total[pl.ds(pl.multiple_of(cut + z * 64, 64), 64)]
        arrive(copies)
        a = ya[0].astype(F32)
        for k in range(1, NY):
            a = a + ya[k].astype(F32)
        a = a.astype(BF16)
        for k in range(NZ):
            a2[k] = a[k * 16:(k + 1) * 16]
        b = zb[0].astype(F32)
        for k in range(1, NZ):
            b = b + zb[k].astype(F32)
        b = b.astype(BF16)
        for k in range(NY):
            b2[k] = b[(k // 2) * 16:(k // 2 + 1) * 16, (k % 2) * 128:(k % 2 + 1) * 128]
        copies = []
        for k in order_8:
            copies.append(send(b2.at[lax.rem(y + k, NY)], yb.at[y], to_y(k)))
            if k in order_4:
                copies.append(send(a2.at[lax.rem(z + k, NZ)], za.at[z], to_z(k)))
        ride(2, copies)
        za[z] = a2[z]
        yb[y] = b2[y]
        arrive(copies)
        a = za[0].astype(F32)
        for k in range(1, NZ):
            a = a + za[k].astype(F32)
        b = yb[0].astype(F32)
        for k in range(1, NY):
            b = b + yb[k].astype(F32)
        return a, b

    a_row = pl.multiple_of(y * 64 + z * 16, 16)
    b_row = pl.multiple_of(512 + z * 64 + (y // 2) * 16, 16)
    b_lane = pl.multiple_of(lax.rem(y, 2) * 128, 128)

    def gather_rows(full, a, b):
        at_a = full.at[core, pl.ds(a_row, 16)]
        at_b = full.at[core, pl.ds(b_row, 16), pl.ds(b_lane, 128)]
        at_a[...] = a
        at_b[...] = b
        copies = []
        for k in order_8:
            copies.append(send(at_b, at_b, to_y(k)))
            if k in order_4:
                copies.append(send(at_a, at_a, to_z(k)))
        arrive(copies)
        at_a = full.at[core, pl.ds(pl.multiple_of(y * 64, 64), 64)]
        at_b = full.at[core, pl.ds(pl.multiple_of(512 + z * 64, 64), 64)]
        copies = []
        for k in order_8:
            copies.append(send(at_a, at_a, to_y(k)))
            if k in order_4:
                copies.append(send(at_b, at_b, to_z(k)))
        arrive(copies)
        return [send(full.at[core], full.at[core], partner)]

    a, b = reduce_rows(err, g_keep, g_out, g_in, g_sum, g_ya, g_zb, g_a2, g_b2, g_za, g_yb, lambda *_: None)
    lane = pl.multiple_of(core * half, half)
    a = a + DAMPING * w_ref[pl.ds(a_row, 16), pl.ds(lane, half)].astype(F32)
    b = b + DAMPING * w_ref[pl.ds(b_row, 16), pl.ds(pl.multiple_of(core * half + b_lane, 128), 128)].astype(F32)
    grad_a[...] = a
    grad_b[...] = b
    copies = gather_rows(grad, a.astype(BF16), b.astype(BF16))
    norm = jnp.sum(jnp.sum(a * a, axis=1, keepdims=True), axis=0, keepdims=True) + jnp.sum(
        jnp.sum(b * b, axis=1, keepdims=True), axis=0, keepdims=True)

    def project(side):
        value = jnp.dot(x_ref[...], grad[side], preferred_element_type=F32).astype(BF16)
        proj[side] = value.reshape(proj.shape[1:])
        return [send(proj.at[side, lax.rem(feat + k, NF)], got_p.at[side, feat], to_feat(k)) for k in order_8]

    first = project(core)
    arrive(copies)
    second = project(1 - core)
    got_p[0, feat] = proj[0, feat]
    got_p[1, feat] = proj[1, feat]
    arrive(first + second)
    pj = []
    for side in range(2):
        value = got_p[side, 0].astype(F32)
        for k in range(1, NF):
            value = value + got_p[side, k].astype(F32)
        pj.append(value)
    p0, p1 = probs[:, :half], probs[:, half:]
    pp0, pp1 = p0 * pj[0], p1 * pj[1]
    inner = jnp.sum(pp0, axis=1, keepdims=True) + jnp.sum(pp1, axis=1, keepdims=True)
    scale = count / total_samples
    w0 = ((pp0 - p0 * inner) * scale).astype(BF16)
    w1 = ((pp1 - p1 * inner) * scale).astype(BF16)
    wgt[0, feat] = w0
    wgt[1, feat] = w1
    copies = [send(wgt.at[:, feat], wgt.at[:, feat], to_feat(k)) for k in order_8]
    curv = jnp.sum(jnp.sum(w0.astype(F32) * pj[0] + w1.astype(F32) * pj[1], axis=1, keepdims=True), axis=0, keepdims=True)
    top = lax.broadcasted_iota(jnp.int32, (8, 128), 0) < 4
    sc_f[feat] = jnp.where(top, norm, curv)
    copies += [send(sc_f.at[feat], sc_f.at[feat], to_feat(k)) for k in order_8]
    arrive(copies)

    def ride(stage, copies):
        if stage == 0:
            sc_c[core] = functools.reduce(jnp.add, [sc_f[k] for k in range(NF)])
            copies += [send(sc_c.at[core], sc_c.at[core], partner)]
        if stage == 1:
            sc_y[y] = sc_c[0] + sc_c[1]
            copies += [send(sc_y.at[y], sc_y.at[y], to_y(k)) for k in order_8]
        if stage == 2:
            sc_z[z] = functools.reduce(jnp.add, [sc_y[k] for k in range(NY)])
            copies += [send(sc_z.at[z], sc_z.at[z], to_z(k)) for k in order_4]

    a, b = reduce_rows(wgt, i_keep, i_out, i_in, i_sum, i_ya, i_zb, i_a2, i_b2, i_za, i_yb, ride)
    sums = functools.reduce(jnp.add, [sc_z[k] for k in range(NZ)])
    norm, curv = sums[0:1, 0:1], sums[4:5, 0:1]
    alpha = norm / (curv + DAMPING * norm)
    a = -grad_a[...] + alpha * (a + DAMPING * grad_a[...])
    b = -grad_b[...] + alpha * (b + DAMPING * grad_b[...])
    copies = gather_rows(resid, a.astype(BF16), b.astype(BF16))
    step_ref[:, :half] = (-alpha * grad[0].astype(F32)).astype(BF16)
    step_ref[:, half:] = (-alpha * grad[1].astype(F32)).astype(BF16)
    arrive(copies)
    res_ref[:, :half] = resid[0]
    res_ref[:, half:] = resid[1]
    for copy in pending:
        copy.wait_send()


def body(features, labels, probe_weight, sampled):
    height, depth = features.shape
    classes = probe_weight.shape[1]
    half = classes // 2
    own = height // NF
    vmem = pl.BlockSpec(memory_space=pltpu.VMEM)
    out = jax.ShapeDtypeStruct((depth, classes), BF16)

    def chain():
        return [
            pltpu.VMEM((depth, half), F32),
            pltpu.VMEM((depth, half), BF16),
            pltpu.VMEM((depth, half), BF16),
            pltpu.VMEM((depth, half), BF16),
            pltpu.VMEM((NY, 64, half), BF16),
            pltpu.VMEM((NZ, 64, half), BF16),
            pltpu.VMEM((NZ, 16, half), BF16),
            pltpu.VMEM((NY, 16, 128), BF16),
            pltpu.VMEM((NZ, 16, half), BF16),
            pltpu.VMEM((NY, 16, 128), BF16),
        ]

    return pl.pallas_call(
        kernel,
        out_shape=(out, out),
        in_specs=[vmem] * 4,
        out_specs=(vmem, vmem),
        scratch_shapes=[
            pltpu.VMEM((depth, height), BF16),
            pltpu.VMEM((NF, own, classes), F32),
            pltpu.VMEM((NF, own, classes), F32),
            pltpu.VMEM((2, NF, own, half), BF16),
            pltpu.VMEM((own, classes), F32),
            *chain(),
            pltpu.VMEM((16, half), F32),
            pltpu.VMEM((16, 128), F32),
            pltpu.VMEM((2, depth, half), BF16),
            pltpu.VMEM((2, NF, own, half), BF16),
            pltpu.VMEM((2, NF, own, half), BF16),
            pltpu.VMEM((2, NF, own, half), BF16),
            *chain(),
            pltpu.VMEM((2, depth, half), BF16),
            pltpu.VMEM((NF, 8, 128), F32),
            pltpu.VMEM((2, 8, 128), F32),
            pltpu.VMEM((NY, 8, 128), F32),
            pltpu.VMEM((NZ, 8, 128), F32),
            pltpu.SemaphoreType.DMA((160,)),
            pltpu.SemaphoreType.DMA((160,)),
        ],
        compiler_params=pltpu.CompilerParams(
            collective_id=0, has_side_effects=True, vmem_limit_bytes=40 * 1024 * 1024
        ),
    )(features, labels.reshape(1, height), probe_weight, sampled.reshape(1, sampled.shape[0]))


def solution(mesh):
    in_specs = (P("rows", "feat"), P("rows"), P("feat", None), P("rows"))
    out_specs = (P("feat", None), P("feat", None))
    return jax.shard_map(body, mesh=mesh, in_specs=in_specs, out_specs=out_specs, check_vma=False)
```

```python
import functools

import jax
import jax.numpy as jnp
from jax import lax
from jax.experimental import pallas as pl
from jax.experimental.pallas import tpu as pltpu
from jax.sharding import PartitionSpec as P

MESH = pl.DeviceIdType.MESH
DAMPING = 0.01
F32, BF16 = jnp.float32, jnp.bfloat16
NF, NZ, NY, LANES = 8, 4, 8, 128
VMEM_BYTES = 56 * 1024 * 1024
ORDER_8, ORDER_4 = (4, 3, 5, 2, 6, 1, 7), (2, 1, 3)


def add_all(values):
    return functools.reduce(jnp.add, values)


def total_of(value):
    return jnp.sum(jnp.sum(value, axis=1, keepdims=True), axis=0, keepdims=True)


def kernel(x_hbm, lab_hbm, w_hbm, smp_hbm, step_out, resid_out, step_ref, resid, x_ref, lab_ref, w_ref, smp_ref, xt, part, got_l, err, probs,
           g_keep, g_out, g_in, g_sum, g_y, g_z, grad_own, grad, proj, got_p, wgt, i_keep, i_out, i_in, i_sum, i_y, i_z,
           sc_f, sc_c, sc_y, sc_z, loads, stores, sends, recvs):
    rows = lax.axis_index("rows")
    feat = lax.axis_index("feat")
    core = lax.rem(rows, 2)
    y = lax.rem(rows // 2, NY)
    z = rows // (2 * NY)
    height, depth = x_ref.shape
    own = height // NF
    half = w_ref.shape[1] // 2
    piece = depth // NY
    total_rows = height * NF * 8
    total_samples = smp_ref.shape[1] * NF * 8

    loaded = [pltpu.make_async_copy(src, dst, loads.at[i]) for i, (src, dst) in enumerate(
        ((x_hbm, x_ref), (w_hbm, w_ref), (lab_hbm, lab_ref), (smp_hbm, smp_ref)))]
    for copy in loaded:
        copy.start()

    def to_feat(k):
        return {"rows": rows, "feat": lax.rem(feat + k, NF)}

    def to_y(k):
        return {"rows": (z * NY + lax.rem(y + k, NY)) * 2 + core, "feat": feat}

    def to_z(k):
        return {"rows": (lax.rem(z + k, NZ) * NY + y) * 2 + core, "feat": feat}

    partner = {"rows": rows + 1 - 2 * core, "feat": feat}
    pending = []

    def send(src, dst, where):
        index = len(pending)
        copy = pltpu.make_async_remote_copy(
            src_ref=src, dst_ref=dst, send_sem=sends.at[index], recv_sem=recvs.at[index], device_id=where,
            device_id_type=MESH,
        )
        copy.start()
        pending.append(copy)
        return copy

    def arrive(copies):
        for copy in copies:
            copy.wait_recv()

    barrier = pltpu.get_barrier_semaphore()
    peers = [partner] + [to_feat(k) for k in ORDER_8] + [to_y(k) for k in ORDER_8] + [to_z(k) for k in ORDER_4]
    for where in peers:
        pl.semaphore_signal(barrier, inc=1, device_id=where, device_id_type=MESH)

    loaded[0].wait()
    loaded[1].wait()
    copies = []
    for side in range(2):
        part[side] = jnp.dot(
            x_ref[...], w_ref[:, side * half:(side + 1) * half], preferred_element_type=F32).reshape(part.shape[1:])
        if side == 0:
            pl.semaphore_wait(barrier, len(peers))
        copies += [send(part.at[side, lax.rem(feat + k, NF)], got_l.at[side, feat], to_feat(k)) for k in ORDER_8]
    xt[...] = x_ref[...].T
    loaded[2].wait()
    loaded[3].wait()
    row_id = feat * own + lax.broadcasted_iota(jnp.int32, (own, height), 0)
    here = row_id == lax.broadcasted_iota(jnp.int32, (own, height), 1)
    label = jnp.sum(jnp.where(here, lab_ref[...], 0), axis=1, keepdims=True)
    sample_id = feat * own + lax.broadcasted_iota(jnp.int32, (own, smp_ref.shape[1]), 0)
    count = jnp.sum(jnp.where(sample_id == smp_ref[...], 1.0, 0.0), axis=1, keepdims=True)
    for side in range(2):
        got_l[side, feat] = part[side, feat]
    arrive(copies)
    logits = [add_all([got_l[side, k] for k in range(NF)]) for side in range(2)]
    highest = jnp.max(jnp.maximum(*logits), axis=1, keepdims=True)
    expo = [jnp.exp(value - highest) for value in logits]
    bottom = jnp.sum(expo[0] + expo[1], axis=1, keepdims=True)
    for side in range(2):
        p = expo[side] / bottom
        probs[side] = p
        class_id = side * half + lax.broadcasted_iota(jnp.int32, p.shape, 1)
        err[side, feat] = ((p - jnp.where(label == class_id, 1.0, 0.0)) / total_rows).astype(BF16)
    arrive([send(err.at[:, feat], err.at[:, feat], to_feat(k)) for k in ORDER_8])

    def reduce_rows(mat, keep, out, into, total, by_y, by_z, ride):
        value = jnp.dot(xt[...], mat[1 - core].reshape(height, half), preferred_element_type=F32).astype(BF16)
        copies = []
        for j in range(2):
            out[j] = value[:, j * LANES:(j + 1) * LANES]
            copies.append([send(out.at[j], into.at[j], partner)])
        extra = ride(0, None)
        keep[...] = jnp.dot(xt[...], mat[core].reshape(height, half), preferred_element_type=F32)
        along_y = []
        for j in range(2):
            arrive(copies[j])
            total[j] = (keep[:, j * LANES:(j + 1) * LANES] + into[j].astype(F32)).astype(BF16)
            moves = []
            for k in ORDER_8:
                there = pl.multiple_of(lax.rem(y + k, NY) * piece, piece)
                moves.append(send(total.at[j, pl.ds(there, piece)], by_y.at[j, y], to_y(k)))
            by_y[j, y] = total[j, pl.ds(pl.multiple_of(y * piece, piece), piece)]
            along_y.append(moves)
        extra = ride(1, extra)
        along_z = []
        for j in range(2):
            arrive(along_y[j])
            by_z[j, z] = add_all([by_y[j, k].astype(F32) for k in range(NY)]).astype(BF16)
            along_z.append([send(by_z.at[j, z], by_z.at[j, z], to_z(k)) for k in ORDER_4])
        extra = ride(2, extra)
        for j in range(2):
            arrive(along_z[j])
            if j == 0:
                ride(3, extra)
            yield add_all([by_z[j, k].astype(F32) for k in range(NZ)])

    my_rows = pl.ds(pl.multiple_of(y * piece, piece), piece)

    def gather_y(full, j, value):
        mine = full.at[core, j, my_rows]
        mine[...] = value
        return [send(mine, mine, to_y(k)) for k in ORDER_8]

    def across(full, j):
        return [send(full.at[core, j], full.at[core, j], partner)]

    norm = jnp.zeros((1, 1), F32)
    gathers = []
    for j, value in enumerate(reduce_rows(err, g_keep, g_out, g_in, g_sum, g_y, g_z, lambda *_: None)):
        lane = pl.multiple_of(core * half + j * LANES, LANES)
        value = value + DAMPING * w_ref[my_rows, pl.ds(lane, LANES)].astype(F32)
        gathers.append(gather_y(grad, j, value.astype(BF16)))
        grad_own[j] = value
        norm = norm + total_of(value * value)

    def project(side, j):
        value = jnp.dot(x_ref[...], grad[side, j], preferred_element_type=F32).astype(BF16)
        proj[side, j] = value.reshape(proj.shape[2:])
        return [send(proj.at[side, j, lax.rem(feat + k, NF)], got_p.at[side, j, feat], to_feat(k)) for k in ORDER_8]

    arrivals = []
    for j in range(2):
        arrive(gathers[j])
        copies = across(grad, j)
        arrivals += project(core, j)
        arrive(copies)
        arrivals += project(1 - core, j)
    for side in range(2):
        for j in range(2):
            got_p[side, j, feat] = proj[side, j, feat]
    arrive(arrivals)
    quarters = [(side, j) for side in range(2) for j in range(2)]
    pj = [add_all([got_p[side, j, k].astype(F32) for k in range(NF)]) for side, j in quarters]
    ps = [probs[side, :, j * LANES:(j + 1) * LANES] for side, j in quarters]
    pp = [a * b for a, b in zip(ps, pj)]
    inner = jnp.sum(add_all(pp), axis=1, keepdims=True)
    scale = count / total_samples
    curv = jnp.zeros((1, 1), F32)
    weighted = [((a - b * inner) * scale).astype(BF16) for a, b in zip(pp, ps)]
    for (side, j), value in zip(quarters, weighted):
        wgt[side, feat, :, j * LANES:(j + 1) * LANES] = value
    copies = [send(wgt.at[:, feat], wgt.at[:, feat], to_feat(k)) for k in ORDER_8]
    curv = total_of(add_all([a.astype(F32) * b for a, b in zip(weighted, pj)]))
    top = lax.broadcasted_iota(jnp.int32, (8, LANES), 0) < 4
    sc_f[feat] = jnp.where(top, norm / NZ, curv)
    scalars = [send(sc_f.at[feat], sc_f.at[feat], to_feat(k)) for k in ORDER_8]
    arrive(copies)

    def ride(stage, copies):
        if stage == 0:
            arrive(scalars)
            sc_c[core] = add_all([sc_f[k] for k in range(NF)])
            return [send(sc_c.at[core], sc_c.at[core], partner)]
        arrive(copies)
        if stage == 1:
            sc_y[y] = sc_c[0] + sc_c[1]
            return [send(sc_y.at[y], sc_y.at[y], to_y(k)) for k in ORDER_8]
        if stage == 2:
            sc_z[z] = add_all([sc_y[k] for k in range(NY)])
            return [send(sc_z.at[z], sc_z.at[z], to_z(k)) for k in ORDER_4]
        return None

    gathers = []
    for j, value in enumerate(reduce_rows(wgt, i_keep, i_out, i_in, i_sum, i_y, i_z, ride)):
        if j == 0:
            sums = add_all([sc_z[k] for k in range(NZ)])
            norm, curv = sums[0:1, 0:1], sums[4:5, 0:1]
            alpha = norm / (curv + DAMPING * norm)
        g = grad_own[j]
        gathers.append(gather_y(resid, j, (-g + alpha * (value + DAMPING * g)).astype(BF16)))
    stored = []

    def store(src, dst, side, j):
        lanes = pl.ds(pl.multiple_of((2 * side + j) * LANES, LANES), LANES)
        copy = pltpu.make_async_copy(src.at[side, j], dst.at[:, lanes], stores.at[len(stored)])
        copy.start()
        stored.append(copy)

    for side, j in quarters:
        step_ref[side, j] = (-alpha * grad[side, j].astype(F32)).astype(BF16)
        store(step_ref, step_out, side, j)
    copies = []
    for j in range(2):
        arrive(gathers[j])
        copies.append(across(resid, j))
        store(resid, resid_out, core, j)
    for j in range(2):
        arrive(copies[j])
        store(resid, resid_out, 1 - core, j)
    for copy in stored:
        copy.wait()
    for copy in pending:
        copy.wait_send()


def write(step_ref, resid_ref, step_out, resid_out, sems):
    copies = []
    depth = step_ref.shape[0]
    for src, dst in ((step_ref, step_out), (resid_ref, resid_out)):
        for part in range(4):
            some = pl.ds(part * (depth // 4), depth // 4)
            copies.append(pltpu.make_async_copy(src.at[some], dst.at[some], sems.at[len(copies)]))
    for copy in copies:
        copy.start()
    for copy in copies:
        copy.wait()


def body(features, labels, probe_weight, sampled):
    height, depth = features.shape
    classes = probe_weight.shape[1]
    half = classes // 2
    own = height // NF
    piece = depth // NY
    hbm = pl.BlockSpec(memory_space=pltpu.HBM)
    out = jax.ShapeDtypeStruct((depth, classes), BF16)
    labels = labels.reshape(1, height)
    sampled = sampled.reshape(1, sampled.shape[0])

    def chain():
        return [
            pltpu.VMEM((depth, half), F32),
            pltpu.VMEM((2, depth, LANES), BF16),
            pltpu.VMEM((2, depth, LANES), BF16),
            pltpu.VMEM((2, depth, LANES), BF16),
            pltpu.VMEM((2, NY, piece, LANES), BF16),
            pltpu.VMEM((2, NZ, piece, LANES), BF16),
        ]

    step, resid = pl.pallas_call(
        kernel,
        out_shape=(out, out),
        in_specs=[hbm] * 4,
        out_specs=(hbm, hbm),
        scratch_shapes=[
            pltpu.VMEM((2, 2, depth, LANES), BF16),
            pltpu.VMEM((2, 2, depth, LANES), BF16),
            pltpu.VMEM(features.shape, BF16),
            pltpu.VMEM(labels.shape, jnp.int32),
            pltpu.VMEM(probe_weight.shape, BF16),
            pltpu.VMEM(sampled.shape, jnp.int32),
            pltpu.VMEM((depth, height), BF16),
            pltpu.VMEM((2, NF, own, half), F32),
            pltpu.VMEM((2, NF, own, half), F32),
            pltpu.VMEM((2, NF, own, half), BF16),
            pltpu.VMEM((2, own, half), F32),
            *chain(),
            pltpu.VMEM((2, piece, LANES), F32),
            pltpu.VMEM((2, 2, depth, LANES), BF16),
            pltpu.VMEM((2, 2, NF, own, LANES), BF16),
            pltpu.VMEM((2, 2, NF, own, LANES), BF16),
            pltpu.VMEM((2, NF, own, half), BF16),
            *chain(),
            pltpu.VMEM((NF, 8, LANES), F32),
            pltpu.VMEM((2, 8, LANES), F32),
            pltpu.VMEM((NY, 8, LANES), F32),
            pltpu.VMEM((NZ, 8, LANES), F32),
            pltpu.SemaphoreType.DMA((4,)),
            pltpu.SemaphoreType.DMA((8,)),
            pltpu.SemaphoreType.DMA((192,)),
            pltpu.SemaphoreType.DMA((192,)),
        ],
        compiler_params=pltpu.CompilerParams(
            collective_id=0, has_side_effects=True, vmem_limit_bytes=VMEM_BYTES
        ),
    )(features, labels, probe_weight, sampled)
    return pl.pallas_call(
        write,
        out_shape=(out, out),
        in_specs=[hbm] * 2,
        out_specs=(hbm, hbm),
        scratch_shapes=[pltpu.SemaphoreType.DMA((8,))],
        compiler_params=pltpu.CompilerParams(vmem_limit_bytes=VMEM_BYTES),
    )(step, resid)


def solution(mesh):
    in_specs = (P("rows", "feat"), P("rows"), P("feat", None), P("rows"))
    out_specs = (P("feat", None), P("feat", None))
    return jax.shard_map(body, mesh=mesh, in_specs=in_specs, out_specs=out_specs, check_vma=False)
```

```python
import functools

import jax
import jax.numpy as jnp
from jax import lax
from jax.experimental import pallas as pl
from jax.experimental.pallas import tpu as pltpu
from jax.sharding import PartitionSpec as P

MESH = pl.DeviceIdType.MESH
DAMPING = 0.01
F32, BF16 = jnp.float32, jnp.bfloat16
NF, NZ, NY, LANES = 8, 4, 8, 128
VMEM_BYTES = 56 * 1024 * 1024
ORDER_8, ORDER_4 = (4, 3, 5, 2, 6, 1, 7), (2, 1, 3)


def add_all(values):
    return functools.reduce(jnp.add, values)


def total_of(value):
    return jnp.sum(jnp.sum(value, axis=1, keepdims=True), axis=0, keepdims=True)


def kernel(x_hbm, lab_hbm, w_hbm, smp_hbm, step_out, resid_out, step_ref, resid, x_ref, lab_ref, w_ref, smp_ref, xt, part, got_l, err, probs,
           g_keep, g_out, g_in, g_sum, g_ya, g_za, g_zb, g_b, g_yb, grad_a, grad_b, grad, pacc, proj, got_p,
           wgt, i_keep, i_out, i_in, i_sum, i_ya, i_za, i_zb, i_b, i_yb,
           sc_f, sc_c, sc_y, sc_z, loads, stores, sends, recvs):
    rows = lax.axis_index("rows")
    feat = lax.axis_index("feat")
    core = lax.rem(rows, 2)
    y = lax.rem(rows // 2, NY)
    z = rows // (2 * NY)
    height, depth = x_ref.shape
    own = height // NF
    half = w_ref.shape[1] // 2
    top = depth * 2 // 3
    pa, pb = top // NY, (depth - top) // NZ
    total_rows = height * NF * 8
    total_samples = smp_ref.shape[1] * NF * 8

    loaded = [pltpu.make_async_copy(src, dst, loads.at[i]) for i, (src, dst) in enumerate(
        ((x_hbm, x_ref), (w_hbm, w_ref), (lab_hbm, lab_ref), (smp_hbm, smp_ref)))]
    for copy in loaded:
        copy.start()

    def to_feat(k):
        return {"rows": rows, "feat": lax.rem(feat + k, NF)}

    def to_y(k):
        return {"rows": (z * NY + lax.rem(y + k, NY)) * 2 + core, "feat": feat}

    def to_z(k):
        return {"rows": (lax.rem(z + k, NZ) * NY + y) * 2 + core, "feat": feat}

    partner = {"rows": rows + 1 - 2 * core, "feat": feat}
    pending = []

    def send(src, dst, where):
        index = len(pending)
        copy = pltpu.make_async_remote_copy(
            src_ref=src, dst_ref=dst, send_sem=sends.at[index], recv_sem=recvs.at[index], device_id=where,
            device_id_type=MESH,
        )
        copy.start()
        pending.append(copy)
        return copy

    def arrive(copies):
        for copy in copies:
            copy.wait_recv()

    barrier = pltpu.get_barrier_semaphore()
    peers = [partner] + [to_feat(k) for k in ORDER_8] + [to_y(k) for k in ORDER_8] + [to_z(k) for k in ORDER_4]
    for where in peers:
        pl.semaphore_signal(barrier, inc=1, device_id=where, device_id_type=MESH)

    loaded[0].wait()
    loaded[1].wait()
    copies = []
    for side in range(2):
        part[side] = jnp.dot(
            x_ref[...], w_ref[:, side * half:(side + 1) * half], preferred_element_type=F32).reshape(part.shape[1:])
        if side == 0:
            pl.semaphore_wait(barrier, len(peers))
        copies += [send(part.at[side, lax.rem(feat + k, NF)], got_l.at[side, feat], to_feat(k)) for k in ORDER_8]
    xt[...] = x_ref[...].T
    loaded[2].wait()
    loaded[3].wait()
    row_id = feat * own + lax.broadcasted_iota(jnp.int32, (own, height), 0)
    here = row_id == lax.broadcasted_iota(jnp.int32, (own, height), 1)
    label = jnp.sum(jnp.where(here, lab_ref[...], 0), axis=1, keepdims=True)
    sample_id = feat * own + lax.broadcasted_iota(jnp.int32, (own, smp_ref.shape[1]), 0)
    count = jnp.sum(jnp.where(sample_id == smp_ref[...], 1.0, 0.0), axis=1, keepdims=True)
    for side in range(2):
        got_l[side, feat] = part[side, feat]
    arrive(copies)
    logits = [add_all([got_l[side, k] for k in range(NF)]) for side in range(2)]
    highest = jnp.max(jnp.maximum(*logits), axis=1, keepdims=True)
    expo = [jnp.exp(value - highest) for value in logits]
    bottom = jnp.sum(expo[0] + expo[1], axis=1, keepdims=True)
    for side in range(2):
        p = expo[side] / bottom
        probs[side] = p
        class_id = side * half + lax.broadcasted_iota(jnp.int32, p.shape, 1)
        err[side, feat] = ((p - jnp.where(label == class_id, 1.0, 0.0)) / total_rows).astype(BF16)
    arrive([send(err.at[:, feat], err.at[:, feat], to_feat(k)) for k in ORDER_8])

    def rows_at(start, size):
        return pl.ds(pl.multiple_of(start, size), size)

    a_rows = rows_at(y * pa, pa)
    b_rows = rows_at(top + z * pb, pb)
    b_side, b_part = lax.rem(y, 2), rows_at(top + z * pb + (y // 2) * 16, 16)
    both, upper, lower = pl.ds(0, 2), pl.ds(0, top), pl.ds(top, depth - top)

    def sum_rows(mat, full, finish, keep, out, into, total, ya, za, zb, b2, yb, ride):
        def times(side, start, stop):
            return jnp.dot(xt[start:stop], mat[side].reshape(height, half), preferred_element_type=F32)

        value = times(1 - core, top, depth).astype(BF16)
        for j in range(2):
            out[j, top:] = value[:, j * LANES:(j + 1) * LANES]
        core_b = [send(out.at[both, lower], into.at[both, lower], partner)]
        value = times(1 - core, 0, top).astype(BF16)
        core_a = []
        for j in range(2):
            out[j, :top] = value[:, j * LANES:(j + 1) * LANES]
            core_a.append([send(out.at[j, upper], into.at[j, upper], partner)])
        extra = ride(0, None)
        for start, stop in ((top, depth), (0, top)):
            value = times(core, start, stop)
            for j in range(2):
                keep[j, start:stop] = value[:, j * LANES:(j + 1) * LANES]
        extra = ride(1, extra)

        arrive(core_b)
        for j in range(2):
            total[j, top:] = (keep[j, top:] + into[j, top:].astype(F32)).astype(BF16)
        to_zb = []
        for k in ORDER_4:
            there = rows_at(top + lax.rem(z + k, NZ) * pb, pb)
            to_zb.append(send(total.at[both, there], zb.at[z], to_z(k)))
        to_ya = []
        for j in range(2):
            arrive(core_a[j])
            total[j, :top] = (keep[j, :top] + into[j, :top].astype(F32)).astype(BF16)
            to_ya.append([send(total.at[j, rows_at(lax.rem(y + k, NY) * pa, pa)], ya.at[j, y], to_y(k)) for k in ORDER_8])
        zb[z] = total[both, b_rows]
        for j in range(2):
            ya[j, y] = total[j, a_rows]

        arrive(to_zb)
        b2[...] = add_all([zb[k].astype(F32) for k in range(NZ)]).astype(BF16)
        to_yb = []
        for k in ORDER_8:
            there = lax.rem(y + k, NY)
            to_yb.append(send(b2.at[lax.rem(there, 2), rows_at((there // 2) * 16, 16)], yb.at[y], to_y(k)))
        yb[y] = b2[b_side, rows_at((y // 2) * 16, 16)]
        to_za = []
        for j in range(2):
            arrive(to_ya[j])
            za[j, z] = add_all([ya[j, k].astype(F32) for k in range(NY)]).astype(BF16)
            to_za.append([send(za.at[j, z], za.at[j, z], to_z(k)) for k in ORDER_4])
            if j == 0:
                extra = ride(2, extra)

        arrive(to_yb)
        ride(3, extra)
        mine = full.at[core, b_side, b_part]
        mine[...] = finish(2, add_all([yb[k].astype(F32) for k in range(NY)])).astype(BF16)
        from_yb = [send(mine, mine, to_y(k)) for k in ORDER_8]
        from_ya = []
        for j in range(2):
            arrive(to_za[j])
            mine = full.at[core, j, a_rows]
            mine[...] = finish(j, add_all([za[j, k].astype(F32) for k in range(NZ)])).astype(BF16)
            from_ya.append([send(mine, mine, to_y(k)) for k in ORDER_8])

        arrive(from_yb)
        mine = full.at[core, both, b_rows]
        from_zb = [send(mine, mine, to_z(k)) for k in ORDER_4]
        across = []
        for j in range(2):
            arrive(from_ya[j])
            mine = full.at[core, j, upper]
            across.append([send(mine, mine, partner)])
            yield core, j, across[j]
        for j in range(2):
            arrive(across[j])
        yield 1 - core, 0, None
        arrive(from_zb)
        mine = full.at[core, both, lower]
        across = [send(mine, mine, partner)]
        yield core, 2, None
        arrive(across)
        yield 1 - core, 2, None

    norms = []

    def damped(part, value):
        if part < 2:
            lane = pl.multiple_of(core * half + part * LANES, LANES)
            value = value + DAMPING * w_ref[a_rows, pl.ds(lane, LANES)].astype(F32)
            grad_a[part] = value
            norms.append(total_of(value * value) / NZ)
        else:
            lane = pl.multiple_of(core * half + b_side * LANES, LANES)
            value = value + DAMPING * w_ref[b_part, pl.ds(lane, LANES)].astype(F32)
            grad_b[...] = value
            norms.append(total_of(value * value))
        return value

    arrivals = []
    for side, part, _ in sum_rows(
            err, grad, damped, g_keep, g_out, g_in, g_sum, g_ya, g_za, g_zb, g_b, g_yb, lambda *_: None):
        here = slice(0, top) if part < 2 else slice(top, depth)
        if part == 0 and _ is not None:
            continue
        mat = jnp.concatenate([grad[side, 0, here], grad[side, 1, here]], axis=1)
        value = jnp.dot(x_ref[:, here], mat, preferred_element_type=F32)
        if part < 2:
            pacc[side] = value
        else:
            proj[side] = (pacc[side] + value).astype(BF16).reshape(proj.shape[1:])
            arrivals += [send(proj.at[side, lax.rem(feat + k, NF)], got_p.at[side, feat], to_feat(k)) for k in ORDER_8]
    norm = add_all(norms)
    for side in range(2):
        got_p[side, feat] = proj[side, feat]
    arrive(arrivals)
    quarters = [(side, j) for side in range(2) for j in range(2)]
    pj = [add_all([got_p[side, k, :, j * LANES:(j + 1) * LANES].astype(F32) for k in range(NF)]) for side, j in quarters]
    ps = [probs[side, :, j * LANES:(j + 1) * LANES] for side, j in quarters]
    pp = [a * b for a, b in zip(ps, pj)]
    inner = jnp.sum(add_all(pp), axis=1, keepdims=True)
    scale = count / total_samples
    weighted = [((a - b * inner) * scale).astype(BF16) for a, b in zip(pp, ps)]
    for (side, j), value in zip(quarters, weighted):
        wgt[side, feat, :, j * LANES:(j + 1) * LANES] = value
    copies = [send(wgt.at[:, feat], wgt.at[:, feat], to_feat(k)) for k in ORDER_8]
    curv = total_of(add_all([a.astype(F32) * b for a, b in zip(weighted, pj)]))
    upper_half = lax.broadcasted_iota(jnp.int32, (8, LANES), 0) < 4
    sc_f[feat] = jnp.where(upper_half, norm, curv)
    scalars = [send(sc_f.at[feat], sc_f.at[feat], to_feat(k)) for k in ORDER_8]
    arrive(copies)

    alpha = []

    def ride(stage, copies):
        if stage == 0:
            arrive(scalars)
            sc_c[core] = add_all([sc_f[k] for k in range(NF)])
            return [send(sc_c.at[core], sc_c.at[core], partner)]
        arrive(copies)
        if stage == 1:
            sc_y[y] = sc_c[0] + sc_c[1]
            return [send(sc_y.at[y], sc_y.at[y], to_y(k)) for k in ORDER_8]
        if stage == 2:
            sc_z[z] = add_all([sc_y[k] for k in range(NY)])
            return [send(sc_z.at[z], sc_z.at[z], to_z(k)) for k in ORDER_4]
        sums = add_all([sc_z[k] for k in range(NZ)])
        alpha.append(sums[0:1, 0:1] / (sums[4:5, 0:1] + DAMPING * sums[0:1, 0:1]))
        return None

    def residual(part, value):
        g = grad_a[part] if part < 2 else grad_b[...]
        return -g + alpha[0] * (value + DAMPING * g)

    stored = []

    def store(src, dst, side, j, here):
        lanes = pl.ds(pl.multiple_of((2 * side + j) * LANES, LANES), LANES)
        copy = pltpu.make_async_copy(src.at[side, j, here], dst.at[here, lanes], stores.at[len(stored)])
        copy.start()
        stored.append(copy)

    first = True
    for side, part, _ in sum_rows(
            wgt, resid, residual, i_keep, i_out, i_in, i_sum, i_ya, i_za, i_zb, i_b, i_yb, ride):
        if first:
            first = False
            for one, j in quarters:
                step_ref[one, j] = (-alpha[0] * grad[one, j].astype(F32)).astype(BF16)
                store(step_ref, step_out, one, j, pl.ds(0, depth))
        if part == 2:
            for j in range(2):
                store(resid, resid_out, side, j, lower)
        elif _ is not None:
            store(resid, resid_out, side, part, upper)
        else:
            for j in range(2):
                store(resid, resid_out, side, j, upper)
    for copy in stored:
        copy.wait()
    for copy in pending:
        copy.wait_send()


def write(step_ref, resid_ref, step_out, resid_out, held, ins, outs):
    depth = step_ref.shape[0]
    loads, stores = [], []
    for n, (src, dst) in enumerate(((step_ref, step_out), (resid_ref, resid_out))):
        for part in range(4):
            some = pl.ds(part * (depth // 4), depth // 4)
            index = len(loads)
            loads.append(pltpu.make_async_copy(src.at[some], held.at[n, some], ins.at[index]))
            stores.append(pltpu.make_async_copy(held.at[n, some], dst.at[some], outs.at[index]))
    for copy in loads:
        copy.start()
    for there, back in zip(loads, stores):
        there.wait()
        back.start()
    for copy in stores:
        copy.wait()


def body(features, labels, probe_weight, sampled):
    height, depth = features.shape
    classes = probe_weight.shape[1]
    half = classes // 2
    own = height // NF
    top = depth * 2 // 3
    pa, pb = top // NY, (depth - top) // NZ
    hbm = pl.BlockSpec(memory_space=pltpu.HBM)
    out = jax.ShapeDtypeStruct((depth, classes), BF16)
    labels = labels.reshape(1, height)
    sampled = sampled.reshape(1, sampled.shape[0])

    def chain():
        return [
            pltpu.VMEM((2, depth, LANES), F32),
            pltpu.VMEM((2, depth, LANES), BF16),
            pltpu.VMEM((2, depth, LANES), BF16),
            pltpu.VMEM((2, depth, LANES), BF16),
            pltpu.VMEM((2, NY, pa, LANES), BF16),
            pltpu.VMEM((2, NZ, pa, LANES), BF16),
            pltpu.VMEM((NZ, 2, pb, LANES), BF16),
            pltpu.VMEM((2, pb, LANES), BF16),
            pltpu.VMEM((NY, 16, LANES), BF16),
        ]

    step, resid = pl.pallas_call(
        kernel,
        out_shape=(out, out),
        in_specs=[hbm] * 4,
        out_specs=(hbm, hbm),
        scratch_shapes=[
            pltpu.VMEM((2, 2, depth, LANES), BF16),
            pltpu.VMEM((2, 2, depth, LANES), BF16),
            pltpu.VMEM(features.shape, BF16),
            pltpu.VMEM(labels.shape, jnp.int32),
            pltpu.VMEM(probe_weight.shape, BF16),
            pltpu.VMEM(sampled.shape, jnp.int32),
            pltpu.VMEM((depth, height), BF16),
            pltpu.VMEM((2, NF, own, half), F32),
            pltpu.VMEM((2, NF, own, half), F32),
            pltpu.VMEM((2, NF, own, half), BF16),
            pltpu.VMEM((2, own, half), F32),
            *chain(),
            pltpu.VMEM((2, pa, LANES), F32),
            pltpu.VMEM((16, LANES), F32),
            pltpu.VMEM((2, 2, depth, LANES), BF16),
            pltpu.VMEM((2, height, half), F32),
            pltpu.VMEM((2, NF, own, half), BF16),
            pltpu.VMEM((2, NF, own, half), BF16),
            pltpu.VMEM((2, NF, own, half), BF16),
            *chain(),
            pltpu.VMEM((NF, 8, LANES), F32),
            pltpu.VMEM((2, 8, LANES), F32),
            pltpu.VMEM((NY, 8, LANES), F32),
            pltpu.VMEM((NZ, 8, LANES), F32),
            pltpu.SemaphoreType.DMA((4,)),
            pltpu.SemaphoreType.DMA((16,)),
            pltpu.SemaphoreType.DMA((192,)),
            pltpu.SemaphoreType.DMA((192,)),
        ],
        compiler_params=pltpu.CompilerParams(
            collective_id=0, has_side_effects=True, vmem_limit_bytes=VMEM_BYTES
        ),
    )(features, labels, probe_weight, sampled)
    return pl.pallas_call(
        write,
        out_shape=(out, out),
        in_specs=[hbm] * 2,
        out_specs=(hbm, hbm),
        scratch_shapes=[
            pltpu.VMEM((2, depth, classes), BF16),
            pltpu.SemaphoreType.DMA((8,)),
            pltpu.SemaphoreType.DMA((8,)),
        ],
        compiler_params=pltpu.CompilerParams(vmem_limit_bytes=VMEM_BYTES),
    )(step, resid)


def solution(mesh):
    in_specs = (P("rows", "feat"), P("rows"), P("feat", None), P("rows"))
    out_specs = (P("feat", None), P("feat", None))
    return jax.shard_map(body, mesh=mesh, in_specs=in_specs, out_specs=out_specs, check_vma=False)
```

```python
import functools

import jax
import jax.numpy as jnp
from jax import lax
from jax.experimental import pallas as pl
from jax.experimental.pallas import tpu as pltpu
from jax.sharding import PartitionSpec as P

MESH = pl.DeviceIdType.MESH
DAMPING = 0.01
F32, BF16 = jnp.float32, jnp.bfloat16
NF, NZ, NY, LANES = 8, 4, 8, 128
VMEM_BYTES = 56 * 1024 * 1024
ORDER_8, ORDER_4 = (4, 3, 5, 2, 6, 1, 7), (2, 1, 3)


def add_all(values):
    return functools.reduce(jnp.add, values)


def total_of(value):
    return jnp.sum(jnp.sum(value, axis=1, keepdims=True), axis=0, keepdims=True)


def kernel(x_hbm, lab_hbm, w_hbm, smp_hbm, step_out, resid_out, step_ref, resid, x_ref, lab_ref, w_ref, smp_ref, xt, part, got_l, err, probs,
           g_keep, g_out, g_in, g_sum, g_ya, g_za, g_zb, g_yb, grad_a, grad_b, grad, pacc, proj, got_p,
           wgt, i_keep, i_out, i_in, i_sum, i_ya, i_za, i_zb, i_yb,
           sc_f, sc_c, sc_y, sc_z, loads, stores, sends, recvs):
    rows = lax.axis_index("rows")
    feat = lax.axis_index("feat")
    core = lax.rem(rows, 2)
    y = lax.rem(rows // 2, NY)
    z = rows // (2 * NY)
    height, depth = x_ref.shape
    own = height // NF
    half = w_ref.shape[1] // 2
    top = depth * 2 // 3
    pa, pb = top // NY, (depth - top) // NZ
    total_rows = height * NF * 8
    total_samples = smp_ref.shape[1] * NF * 8

    loaded = [pltpu.make_async_copy(src, dst, loads.at[i]) for i, (src, dst) in enumerate(
        ((x_hbm, x_ref), (w_hbm, w_ref), (lab_hbm, lab_ref), (smp_hbm, smp_ref)))]
    for copy in loaded:
        copy.start()

    def to_feat(k):
        return {"rows": rows, "feat": lax.rem(feat + k, NF)}

    def to_y(k):
        return {"rows": (z * NY + lax.rem(y + k, NY)) * 2 + core, "feat": feat}

    def to_z(k):
        return {"rows": (lax.rem(z + k, NZ) * NY + y) * 2 + core, "feat": feat}

    partner = {"rows": rows + 1 - 2 * core, "feat": feat}
    pending = []

    def send(src, dst, where):
        index = len(pending)
        copy = pltpu.make_async_remote_copy(
            src_ref=src, dst_ref=dst, send_sem=sends.at[index], recv_sem=recvs.at[index], device_id=where,
            device_id_type=MESH,
        )
        copy.start()
        pending.append(copy)
        return copy

    def arrive(copies):
        for copy in copies:
            copy.wait_recv()

    barrier = pltpu.get_barrier_semaphore()
    peers = [partner] + [to_feat(k) for k in ORDER_8] + [to_y(k) for k in ORDER_8] + [to_z(k) for k in ORDER_4]
    for where in peers:
        pl.semaphore_signal(barrier, inc=1, device_id=where, device_id_type=MESH)

    loaded[0].wait()
    loaded[1].wait()
    copies = []
    for side in range(2):
        part[side] = jnp.dot(
            x_ref[...], w_ref[:, side * half:(side + 1) * half], preferred_element_type=F32).reshape(part.shape[1:])
        if side == 0:
            pl.semaphore_wait(barrier, len(peers))
        copies += [send(part.at[side, lax.rem(feat + k, NF)], got_l.at[side, feat], to_feat(k)) for k in ORDER_8]
    xt[...] = x_ref[...].T
    loaded[2].wait()
    loaded[3].wait()
    row_id = feat * own + lax.broadcasted_iota(jnp.int32, (own, height), 0)
    here = row_id == lax.broadcasted_iota(jnp.int32, (own, height), 1)
    label = jnp.sum(jnp.where(here, lab_ref[...], 0), axis=1, keepdims=True)
    sample_id = feat * own + lax.broadcasted_iota(jnp.int32, (own, smp_ref.shape[1]), 0)
    count = jnp.sum(jnp.where(sample_id == smp_ref[...], 1.0, 0.0), axis=1, keepdims=True)
    for side in range(2):
        got_l[side, feat] = part[side, feat]
    arrive(copies)
    logits = [add_all([got_l[side, k] for k in range(NF)]) for side in range(2)]
    highest = jnp.max(jnp.maximum(*logits), axis=1, keepdims=True)
    expo = [jnp.exp(value - highest) for value in logits]
    bottom = jnp.sum(expo[0] + expo[1], axis=1, keepdims=True)
    for side in range(2):
        p = expo[side] / bottom
        probs[side] = p
        class_id = side * half + lax.broadcasted_iota(jnp.int32, p.shape, 1)
        err[side, feat] = ((p - jnp.where(label == class_id, 1.0, 0.0)) / total_rows).astype(BF16)
    arrive([send(err.at[:, feat], err.at[:, feat], to_feat(k)) for k in ORDER_8])

    def rows_at(start, size):
        return pl.ds(pl.multiple_of(start, size), size)

    a_rows = rows_at(y * pa, pa)
    b_rows = rows_at(top + z * pb, pb)
    both, upper, lower = pl.ds(0, 2), pl.ds(0, top), pl.ds(top, depth - top)

    def sum_rows(mat, full, finish, keep, out, into, total, ya, za, zb, yb, ride):
        def times(side, start, stop):
            return jnp.dot(xt[start:stop], mat[side].reshape(height, half), preferred_element_type=F32)

        value = times(1 - core, top, depth).astype(BF16)
        for j in range(2):
            out[j, top:] = value[:, j * LANES:(j + 1) * LANES]
        core_b = [send(out.at[both, lower], into.at[both, lower], partner)]
        value = times(1 - core, 0, top).astype(BF16)
        core_a = []
        for j in range(2):
            out[j, :top] = value[:, j * LANES:(j + 1) * LANES]
            core_a.append([send(out.at[j, upper], into.at[j, upper], partner)])
        extra = ride(0, None)
        for start, stop in ((top, depth), (0, top)):
            value = times(core, start, stop)
            for j in range(2):
                keep[j, start:stop] = value[:, j * LANES:(j + 1) * LANES]
        extra = ride(1, extra)

        arrive(core_b)
        for j in range(2):
            total[j, top:] = (keep[j, top:] + into[j, top:].astype(F32)).astype(BF16)
        to_zb = []
        for k in ORDER_4:
            there = rows_at(top + lax.rem(z + k, NZ) * pb, pb)
            to_zb.append(send(total.at[both, there], zb.at[z], to_z(k)))
        to_ya = []
        for j in range(2):
            arrive(core_a[j])
            total[j, :top] = (keep[j, :top] + into[j, :top].astype(F32)).astype(BF16)
            to_ya.append([send(total.at[j, rows_at(lax.rem(y + k, NY) * pa, pa)], ya.at[j, y], to_y(k)) for k in ORDER_8])
        zb[z] = total[both, b_rows]
        for j in range(2):
            ya[j, y] = total[j, a_rows]

        arrive(to_zb)
        yb[y] = add_all([zb[k].astype(F32) for k in range(NZ)]).astype(BF16)
        to_yb = [send(yb.at[y], yb.at[y], to_y(k)) for k in ORDER_8]
        to_za = []
        for j in range(2):
            arrive(to_ya[j])
            za[j, z] = add_all([ya[j, k].astype(F32) for k in range(NY)]).astype(BF16)
            to_za.append([send(za.at[j, z], za.at[j, z], to_z(k)) for k in ORDER_4])
            if j == 0:
                extra = ride(2, extra)

        ride(3, extra)
        from_ya = []

        def gather_a(j):
            arrive(to_za[j])
            mine = full.at[core, j, a_rows]
            mine[...] = finish(j, add_all([za[j, k].astype(F32) for k in range(NZ)])).astype(BF16)
            from_ya.append([send(mine, mine, to_y(k)) for k in ORDER_8])

        gather_a(0)
        arrive(to_yb)
        mine = full.at[core, both, b_rows]
        mine[...] = finish(2, add_all([yb[k].astype(F32) for k in range(NY)])).astype(BF16)
        from_zb = [send(mine, mine, to_z(k)) for k in ORDER_4]
        gather_a(1)
        across = []
        for j in range(2):
            arrive(from_ya[j])
            mine = full.at[core, j, upper]
            across.append([send(mine, mine, partner)])
            yield core, j, across[j]
        for j in range(2):
            arrive(across[j])
        yield 1 - core, 0, None
        arrive(from_zb)
        mine = full.at[core, both, lower]
        across = [send(mine, mine, partner)]
        yield core, 2, None
        arrive(across)
        yield 1 - core, 2, None

    norms = []

    def damped(part, value):
        if part < 2:
            lane = pl.multiple_of(core * half + part * LANES, LANES)
            value = value + DAMPING * w_ref[a_rows, pl.ds(lane, LANES)].astype(F32)
            grad_a[part] = value
            norms.append(total_of(value * value) / NZ)
        else:
            lane = pl.multiple_of(core * half, half)
            weight = w_ref[b_rows, pl.ds(lane, half)].astype(F32)
            value = value + DAMPING * jnp.stack([weight[:, :LANES], weight[:, LANES:]])
            grad_b[...] = value
            norms.append(total_of(value[0] * value[0] + value[1] * value[1]) / NY)
        return value

    arrivals = []
    for side, part, _ in sum_rows(
            err, grad, damped, g_keep, g_out, g_in, g_sum, g_ya, g_za, g_zb, g_yb, lambda *_: None):
        here = slice(0, top) if part < 2 else slice(top, depth)
        if part == 0 and _ is not None:
            continue
        mat = jnp.concatenate([grad[side, 0, here], grad[side, 1, here]], axis=1)
        value = jnp.dot(x_ref[:, here], mat, preferred_element_type=F32)
        if part < 2:
            pacc[side] = value
        else:
            proj[side] = (pacc[side] + value).astype(BF16).reshape(proj.shape[1:])
            arrivals += [send(proj.at[side, lax.rem(feat + k, NF)], got_p.at[side, feat], to_feat(k)) for k in ORDER_8]
    norm = add_all(norms)
    for side in range(2):
        got_p[side, feat] = proj[side, feat]
    arrive(arrivals)
    quarters = [(side, j) for side in range(2) for j in range(2)]
    pj = [add_all([got_p[side, k, :, j * LANES:(j + 1) * LANES].astype(F32) for k in range(NF)]) for side, j in quarters]
    ps = [probs[side, :, j * LANES:(j + 1) * LANES] for side, j in quarters]
    pp = [a * b for a, b in zip(ps, pj)]
    inner = jnp.sum(add_all(pp), axis=1, keepdims=True)
    scale = count / total_samples
    weighted = [((a - b * inner) * scale).astype(BF16) for a, b in zip(pp, ps)]
    for (side, j), value in zip(quarters, weighted):
        wgt[side, feat, :, j * LANES:(j + 1) * LANES] = value
    copies = [send(wgt.at[:, feat], wgt.at[:, feat], to_feat(k)) for k in ORDER_8]
    curv = total_of(add_all([a.astype(F32) * b for a, b in zip(weighted, pj)]))
    upper_half = lax.broadcasted_iota(jnp.int32, (8, LANES), 0) < 4
    sc_f[feat] = jnp.where(upper_half, norm, curv)
    scalars = [send(sc_f.at[feat], sc_f.at[feat], to_feat(k)) for k in ORDER_8]
    arrive(copies)

    alpha = []

    def ride(stage, copies):
        if stage == 0:
            arrive(scalars)
            sc_c[core] = add_all([sc_f[k] for k in range(NF)])
            return [send(sc_c.at[core], sc_c.at[core], partner)]
        arrive(copies)
        if stage == 1:
            sc_y[y] = sc_c[0] + sc_c[1]
            return [send(sc_y.at[y], sc_y.at[y], to_y(k)) for k in ORDER_8]
        if stage == 2:
            sc_z[z] = add_all([sc_y[k] for k in range(NY)])
            return [send(sc_z.at[z], sc_z.at[z], to_z(k)) for k in ORDER_4]
        sums = add_all([sc_z[k] for k in range(NZ)])
        alpha.append(sums[0:1, 0:1] / (sums[4:5, 0:1] + DAMPING * sums[0:1, 0:1]))
        return None

    def residual(part, value):
        g = grad_a[part] if part < 2 else grad_b[...]
        return -g + alpha[0] * (value + DAMPING * g)

    stored = []

    def store(src, dst, side, j, here):
        lanes = pl.ds(pl.multiple_of((2 * side + j) * LANES, LANES), LANES)
        copy = pltpu.make_async_copy(src.at[side, j, here], dst.at[here, lanes], stores.at[len(stored)])
        copy.start()
        stored.append(copy)

    first = True
    for side, part, _ in sum_rows(
            wgt, resid, residual, i_keep, i_out, i_in, i_sum, i_ya, i_za, i_zb, i_yb, ride):
        if first:
            first = False
            for one, j in quarters:
                step_ref[one, j] = (-alpha[0] * grad[one, j].astype(F32)).astype(BF16)
                store(step_ref, step_out, one, j, pl.ds(0, depth))
        if part == 2:
            for j in range(2):
                store(resid, resid_out, side, j, lower)
        elif _ is not None:
            store(resid, resid_out, side, part, upper)
        else:
            for j in range(2):
                store(resid, resid_out, side, j, upper)
    for copy in stored:
        copy.wait()
    for copy in pending:
        copy.wait_send()


def write(step_ref, resid_ref, step_out, resid_out, held, ins, outs):
    depth = step_ref.shape[0]
    loads, stores = [], []
    for n, (src, dst) in enumerate(((step_ref, step_out), (resid_ref, resid_out))):
        for part in range(4):
            some = pl.ds(part * (depth // 4), depth // 4)
            index = len(loads)
            loads.append(pltpu.make_async_copy(src.at[some], held.at[n, some], ins.at[index]))
            stores.append(pltpu.make_async_copy(held.at[n, some], dst.at[some], outs.at[index]))
    for copy in loads:
        copy.start()
    for there, back in zip(loads, stores):
        there.wait()
        back.start()
    for copy in stores:
        copy.wait()


def body(features, labels, probe_weight, sampled):
    height, depth = features.shape
    classes = probe_weight.shape[1]
    half = classes // 2
    own = height // NF
    top = depth * 2 // 3
    pa, pb = top // NY, (depth - top) // NZ
    hbm = pl.BlockSpec(memory_space=pltpu.HBM)
    out = jax.ShapeDtypeStruct((depth, classes), BF16)
    labels = labels.reshape(1, height)
    sampled = sampled.reshape(1, sampled.shape[0])

    def chain():
        return [
            pltpu.VMEM((2, depth, LANES), F32),
            pltpu.VMEM((2, depth, LANES), BF16),
            pltpu.VMEM((2, depth, LANES), BF16),
            pltpu.VMEM((2, depth, LANES), BF16),
            pltpu.VMEM((2, NY, pa, LANES), BF16),
            pltpu.VMEM((2, NZ, pa, LANES), BF16),
            pltpu.VMEM((NZ, 2, pb, LANES), BF16),
            pltpu.VMEM((NY, 2, pb, LANES), BF16),
        ]

    step, resid = pl.pallas_call(
        kernel,
        out_shape=(out, out),
        in_specs=[hbm] * 4,
        out_specs=(hbm, hbm),
        scratch_shapes=[
            pltpu.VMEM((2, 2, depth, LANES), BF16),
            pltpu.VMEM((2, 2, depth, LANES), BF16),
            pltpu.VMEM(features.shape, BF16),
            pltpu.VMEM(labels.shape, jnp.int32),
            pltpu.VMEM(probe_weight.shape, BF16),
            pltpu.VMEM(sampled.shape, jnp.int32),
            pltpu.VMEM((depth, height), BF16),
            pltpu.VMEM((2, NF, own, half), F32),
            pltpu.VMEM((2, NF, own, half), F32),
            pltpu.VMEM((2, NF, own, half), BF16),
            pltpu.VMEM((2, own, half), F32),
            *chain(),
            pltpu.VMEM((2, pa, LANES), F32),
            pltpu.VMEM((2, pb, LANES), F32),
            pltpu.VMEM((2, 2, depth, LANES), BF16),
            pltpu.VMEM((2, height, half), F32),
            pltpu.VMEM((2, NF, own, half), BF16),
            pltpu.VMEM((2, NF, own, half), BF16),
            pltpu.VMEM((2, NF, own, half), BF16),
            *chain(),
            pltpu.VMEM((NF, 8, LANES), F32),
            pltpu.VMEM((2, 8, LANES), F32),
            pltpu.VMEM((NY, 8, LANES), F32),
            pltpu.VMEM((NZ, 8, LANES), F32),
            pltpu.SemaphoreType.DMA((4,)),
            pltpu.SemaphoreType.DMA((16,)),
            pltpu.SemaphoreType.DMA((192,)),
            pltpu.SemaphoreType.DMA((192,)),
        ],
        compiler_params=pltpu.CompilerParams(
            collective_id=0, has_side_effects=True, vmem_limit_bytes=VMEM_BYTES
        ),
    )(features, labels, probe_weight, sampled)
    return pl.pallas_call(
        write,
        out_shape=(out, out),
        in_specs=[hbm] * 2,
        out_specs=(hbm, hbm),
        scratch_shapes=[
            pltpu.VMEM((2, depth, classes), BF16),
            pltpu.SemaphoreType.DMA((8,)),
            pltpu.SemaphoreType.DMA((8,)),
        ],
        compiler_params=pltpu.CompilerParams(vmem_limit_bytes=VMEM_BYTES),
    )(step, resid)


def solution(mesh):
    in_specs = (P("rows", "feat"), P("rows"), P("feat", None), P("rows"))
    out_specs = (P("feat", None), P("feat", None))
    return jax.shard_map(body, mesh=mesh, in_specs=in_specs, out_specs=out_specs, check_vma=False)
```

```python
import functools

import jax
import jax.numpy as jnp
from jax import lax
from jax.experimental import pallas as pl
from jax.experimental.pallas import tpu as pltpu
from jax.sharding import PartitionSpec as P

MESH = pl.DeviceIdType.MESH
DAMPING = 0.01
F32, BF16 = jnp.float32, jnp.bfloat16
NF, NZ, NY, LANES = 8, 4, 8, 128
VMEM_BYTES = 56 * 1024 * 1024
ORDER_8, ORDER_4 = (4, 3, 5, 2, 6, 1, 7), (2, 1, 3)


def add_all(values):
    return functools.reduce(jnp.add, values)


def total_of(value):
    return jnp.sum(jnp.sum(value, axis=1, keepdims=True), axis=0, keepdims=True)


def kernel(x_hbm, lab_hbm, w_hbm, smp_hbm, step_out, resid_out, step_ref, resid, x_ref, lab_ref, w_ref, smp_ref, xt, part, got_l, err, probs,
           g_keep, g_out, g_in, g_sum, g_ya, g_za, g_zb, g_yb, grad_a, grad_b, grad, pacc, proj, got_p,
           wgt, i_keep, i_out, i_in, i_sum, i_ya, i_za, i_zb, i_yb,
           sc_f, sc_c, sc_y, sc_z, loads, stores, sends, recvs):
    rows = lax.axis_index("rows")
    feat = lax.axis_index("feat")
    core = lax.rem(rows, 2)
    y = lax.rem(rows // 2, NY)
    z = rows // (2 * NY)
    height, depth = x_ref.shape
    own = height // NF
    half = w_ref.shape[1] // 2
    top = depth * 2 // 3
    pa, pb = top // NY, (depth - top) // NZ
    total_rows = height * NF * 8
    total_samples = smp_ref.shape[1] * NF * 8

    loaded = [pltpu.make_async_copy(src, dst, loads.at[i]) for i, (src, dst) in enumerate(
        ((x_hbm, x_ref), (w_hbm, w_ref), (lab_hbm, lab_ref), (smp_hbm, smp_ref)))]
    for copy in loaded:
        copy.start()

    def to_feat(k):
        return {"rows": rows, "feat": lax.rem(feat + k, NF)}

    def to_y(k):
        return {"rows": (z * NY + lax.rem(y + k, NY)) * 2 + core, "feat": feat}

    def to_z(k):
        return {"rows": (lax.rem(z + k, NZ) * NY + y) * 2 + core, "feat": feat}

    partner = {"rows": rows + 1 - 2 * core, "feat": feat}
    pending = []

    def send(src, dst, where):
        index = len(pending)
        copy = pltpu.make_async_remote_copy(
            src_ref=src, dst_ref=dst, send_sem=sends.at[index], recv_sem=recvs.at[index], device_id=where,
            device_id_type=MESH,
        )
        copy.start()
        pending.append(copy)
        return copy

    def arrive(copies):
        for copy in copies:
            copy.wait_recv()

    barrier = pltpu.get_barrier_semaphore()
    peers = [partner] + [to_feat(k) for k in ORDER_8] + [to_y(k) for k in ORDER_8] + [to_z(k) for k in ORDER_4]
    for where in peers:
        pl.semaphore_signal(barrier, inc=1, device_id=where, device_id_type=MESH)

    loaded[0].wait()
    loaded[1].wait()
    copies = []
    for side in range(2):
        part[side] = jnp.dot(
            x_ref[...], w_ref[:, side * half:(side + 1) * half], preferred_element_type=F32).reshape(part.shape[1:])
        if side == 0:
            pl.semaphore_wait(barrier, len(peers))
        copies += [send(part.at[side, lax.rem(feat + k, NF)], got_l.at[side, feat], to_feat(k)) for k in ORDER_8]
    xt[...] = x_ref[...].T
    loaded[2].wait()
    loaded[3].wait()
    row_id = feat * own + lax.broadcasted_iota(jnp.int32, (own, height), 0)
    here = row_id == lax.broadcasted_iota(jnp.int32, (own, height), 1)
    label = jnp.sum(jnp.where(here, lab_ref[...], 0), axis=1, keepdims=True)
    sample_id = feat * own + lax.broadcasted_iota(jnp.int32, (own, smp_ref.shape[1]), 0)
    count = jnp.sum(jnp.where(sample_id == smp_ref[...], 1.0, 0.0), axis=1, keepdims=True)
    for side in range(2):
        got_l[side, feat] = part[side, feat]
    arrive(copies)
    logits = [add_all([got_l[side, k] for k in range(NF)]) for side in range(2)]
    highest = jnp.max(jnp.maximum(*logits), axis=1, keepdims=True)
    expo = [jnp.exp(value - highest) for value in logits]
    bottom = jnp.sum(expo[0] + expo[1], axis=1, keepdims=True)
    for side in range(2):
        p = expo[side] / bottom
        probs[side] = p
        class_id = side * half + lax.broadcasted_iota(jnp.int32, p.shape, 1)
        err[side, feat] = ((p - jnp.where(label == class_id, 1.0, 0.0)) / total_rows).astype(BF16)
    arrive([send(err.at[:, feat], err.at[:, feat], to_feat(k)) for k in ORDER_8])

    def rows_at(start, size):
        return pl.ds(pl.multiple_of(start, size), size)

    a_rows = rows_at(y * pa, pa)
    b_rows = rows_at(top + z * pb, pb)
    both, upper, lower = pl.ds(0, 2), pl.ds(0, top), pl.ds(top, depth - top)

    def sum_rows(mat, full, finish, keep, out, into, total, ya, za, zb, yb, ride):
        def times(side, start, stop):
            return jnp.dot(xt[start:stop], mat[side].reshape(height, half), preferred_element_type=F32)

        value = times(1 - core, 0, top).astype(BF16)
        core_a = []
        for j in range(2):
            out[j, :top] = value[:, j * LANES:(j + 1) * LANES]
            core_a.append([send(out.at[j, upper], into.at[j, upper], partner)])
        value = times(1 - core, top, depth).astype(BF16)
        for j in range(2):
            out[j, top:] = value[:, j * LANES:(j + 1) * LANES]
        core_b = [send(out.at[both, lower], into.at[both, lower], partner)]
        extra = ride(0, None)
        for start, stop in ((0, top), (top, depth)):
            value = times(core, start, stop)
            for j in range(2):
                keep[j, start:stop] = value[:, j * LANES:(j + 1) * LANES]
        extra = ride(1, extra)

        to_ya = []
        for j in range(2):
            arrive(core_a[j])
            total[j, :top] = (keep[j, :top] + into[j, :top].astype(F32)).astype(BF16)
            to_ya.append([send(total.at[j, rows_at(lax.rem(y + k, NY) * pa, pa)], ya.at[j, y], to_y(k)) for k in ORDER_8])
        arrive(core_b)
        for j in range(2):
            total[j, top:] = (keep[j, top:] + into[j, top:].astype(F32)).astype(BF16)
        to_zb = []
        for k in ORDER_4:
            there = rows_at(top + lax.rem(z + k, NZ) * pb, pb)
            to_zb.append(send(total.at[both, there], zb.at[z], to_z(k)))
        zb[z] = total[both, b_rows]
        for j in range(2):
            ya[j, y] = total[j, a_rows]

        arrive(to_zb)
        yb[y] = add_all([zb[k].astype(F32) for k in range(NZ)]).astype(BF16)
        to_yb = [send(yb.at[y], yb.at[y], to_y(k)) for k in ORDER_8]
        to_za = []
        for j in range(2):
            arrive(to_ya[j])
            za[j, z] = add_all([ya[j, k].astype(F32) for k in range(NY)]).astype(BF16)
            to_za.append([send(za.at[j, z], za.at[j, z], to_z(k)) for k in ORDER_4])
            if j == 0:
                extra = ride(2, extra)

        ride(3, extra)
        from_ya = []

        def gather_a(j):
            arrive(to_za[j])
            mine = full.at[core, j, a_rows]
            mine[...] = finish(j, add_all([za[j, k].astype(F32) for k in range(NZ)])).astype(BF16)
            from_ya.append([send(mine, mine, to_y(k)) for k in ORDER_8])

        gather_a(0)
        arrive(to_yb)
        mine = full.at[core, both, b_rows]
        mine[...] = finish(2, add_all([yb[k].astype(F32) for k in range(NY)])).astype(BF16)
        from_zb = [send(mine, mine, to_z(k)) for k in ORDER_4]
        gather_a(1)
        across = []
        for j in range(2):
            arrive(from_ya[j])
            mine = full.at[core, j, upper]
            across.append([send(mine, mine, partner)])
            yield core, j, across[j]
        for j in range(2):
            arrive(across[j])
        yield 1 - core, 0, None
        arrive(from_zb)
        mine = full.at[core, both, lower]
        across = [send(mine, mine, partner)]
        yield core, 2, None
        arrive(across)
        yield 1 - core, 2, None

    norms = []

    def damped(part, value):
        if part < 2:
            lane = pl.multiple_of(core * half + part * LANES, LANES)
            value = value + DAMPING * w_ref[a_rows, pl.ds(lane, LANES)].astype(F32)
            grad_a[part] = value
            norms.append(total_of(value * value) / NZ)
        else:
            lane = pl.multiple_of(core * half, half)
            weight = w_ref[b_rows, pl.ds(lane, half)].astype(F32)
            value = value + DAMPING * jnp.stack([weight[:, :LANES], weight[:, LANES:]])
            grad_b[...] = value
            norms.append(total_of(value[0] * value[0] + value[1] * value[1]) / NY)
        return value

    arrivals = []
    for side, part, _ in sum_rows(
            err, grad, damped, g_keep, g_out, g_in, g_sum, g_ya, g_za, g_zb, g_yb, lambda *_: None):
        here = slice(0, top) if part < 2 else slice(top, depth)
        if part == 0 and _ is not None:
            continue
        mat = jnp.concatenate([grad[side, 0, here], grad[side, 1, here]], axis=1)
        value = jnp.dot(x_ref[:, here], mat, preferred_element_type=F32)
        if part < 2:
            pacc[side] = value
        else:
            proj[side] = (pacc[side] + value).astype(BF16).reshape(proj.shape[1:])
            arrivals += [send(proj.at[side, lax.rem(feat + k, NF)], got_p.at[side, feat], to_feat(k)) for k in ORDER_8]
    norm = add_all(norms)
    for side in range(2):
        got_p[side, feat] = proj[side, feat]
    arrive(arrivals)
    quarters = [(side, j) for side in range(2) for j in range(2)]
    pj = [add_all([got_p[side, k, :, j * LANES:(j + 1) * LANES].astype(F32) for k in range(NF)]) for side, j in quarters]
    ps = [probs[side, :, j * LANES:(j + 1) * LANES] for side, j in quarters]
    pp = [a * b for a, b in zip(ps, pj)]
    inner = jnp.sum(add_all(pp), axis=1, keepdims=True)
    scale = count / total_samples
    weighted = [((a - b * inner) * scale).astype(BF16) for a, b in zip(pp, ps)]
    for (side, j), value in zip(quarters, weighted):
        wgt[side, feat, :, j * LANES:(j + 1) * LANES] = value
    copies = [send(wgt.at[:, feat], wgt.at[:, feat], to_feat(k)) for k in ORDER_8]
    curv = total_of(add_all([a.astype(F32) * b for a, b in zip(weighted, pj)]))
    upper_half = lax.broadcasted_iota(jnp.int32, (8, LANES), 0) < 4
    sc_f[feat] = jnp.where(upper_half, norm, curv)
    scalars = [send(sc_f.at[feat], sc_f.at[feat], to_feat(k)) for k in ORDER_8]
    arrive(copies)

    alpha = []

    def ride(stage, copies):
        if stage == 0:
            arrive(scalars)
            sc_c[core] = add_all([sc_f[k] for k in range(NF)])
            return [send(sc_c.at[core], sc_c.at[core], partner)]
        arrive(copies)
        if stage == 1:
            sc_y[y] = sc_c[0] + sc_c[1]
            return [send(sc_y.at[y], sc_y.at[y], to_y(k)) for k in ORDER_8]
        if stage == 2:
            sc_z[z] = add_all([sc_y[k] for k in range(NY)])
            return [send(sc_z.at[z], sc_z.at[z], to_z(k)) for k in ORDER_4]
        sums = add_all([sc_z[k] for k in range(NZ)])
        alpha.append(sums[0:1, 0:1] / (sums[4:5, 0:1] + DAMPING * sums[0:1, 0:1]))
        return None

    def residual(part, value):
        g = grad_a[part] if part < 2 else grad_b[...]
        return -g + alpha[0] * (value + DAMPING * g)

    stored = []

    def store(src, dst, side, j, here):
        lanes = pl.ds(pl.multiple_of((2 * side + j) * LANES, LANES), LANES)
        copy = pltpu.make_async_copy(src.at[side, j, here], dst.at[here, lanes], stores.at[len(stored)])
        copy.start()
        stored.append(copy)

    first = True
    for side, part, _ in sum_rows(
            wgt, resid, residual, i_keep, i_out, i_in, i_sum, i_ya, i_za, i_zb, i_yb, ride):
        if first:
            first = False
            for one, j in quarters:
                step_ref[one, j] = (-alpha[0] * grad[one, j].astype(F32)).astype(BF16)
                store(step_ref, step_out, one, j, pl.ds(0, depth))
        if part == 2:
            for j in range(2):
                store(resid, resid_out, side, j, lower)
        elif _ is not None:
            store(resid, resid_out, side, part, upper)
        else:
            for j in range(2):
                store(resid, resid_out, side, j, upper)
    for copy in stored:
        copy.wait()
    for copy in pending:
        copy.wait_send()


def write(step_ref, resid_ref, step_out, resid_out, held, ins, outs):
    depth = step_ref.shape[0]
    loads, stores = [], []
    for n, (src, dst) in enumerate(((step_ref, step_out), (resid_ref, resid_out))):
        for part in range(8):
            some = pl.ds(part * (depth // 8), depth // 8)
            index = len(loads)
            loads.append(pltpu.make_async_copy(src.at[some], held.at[n, some], ins.at[index]))
            stores.append(pltpu.make_async_copy(held.at[n, some], dst.at[some], outs.at[index]))
    for copy in loads:
        copy.start()
    for there, back in zip(loads, stores):
        there.wait()
        back.start()
    for copy in stores:
        copy.wait()


def body(features, labels, probe_weight, sampled):
    height, depth = features.shape
    classes = probe_weight.shape[1]
    half = classes // 2
    own = height // NF
    top = depth * 2 // 3
    pa, pb = top // NY, (depth - top) // NZ
    hbm = pl.BlockSpec(memory_space=pltpu.HBM)
    out = jax.ShapeDtypeStruct((depth, classes), BF16)
    labels = labels.reshape(1, height)
    sampled = sampled.reshape(1, sampled.shape[0])

    def chain():
        return [
            pltpu.VMEM((2, depth, LANES), F32),
            pltpu.VMEM((2, depth, LANES), BF16),
            pltpu.VMEM((2, depth, LANES), BF16),
            pltpu.VMEM((2, depth, LANES), BF16),
            pltpu.VMEM((2, NY, pa, LANES), BF16),
            pltpu.VMEM((2, NZ, pa, LANES), BF16),
            pltpu.VMEM((NZ, 2, pb, LANES), BF16),
            pltpu.VMEM((NY, 2, pb, LANES), BF16),
        ]

    step, resid = pl.pallas_call(
        kernel,
        out_shape=(out, out),
        in_specs=[hbm] * 4,
        out_specs=(hbm, hbm),
        scratch_shapes=[
            pltpu.VMEM((2, 2, depth, LANES), BF16),
            pltpu.VMEM((2, 2, depth, LANES), BF16),
            pltpu.VMEM(features.shape, BF16),
            pltpu.VMEM(labels.shape, jnp.int32),
            pltpu.VMEM(probe_weight.shape, BF16),
            pltpu.VMEM(sampled.shape, jnp.int32),
            pltpu.VMEM((depth, height), BF16),
            pltpu.VMEM((2, NF, own, half), F32),
            pltpu.VMEM((2, NF, own, half), F32),
            pltpu.VMEM((2, NF, own, half), BF16),
            pltpu.VMEM((2, own, half), F32),
            *chain(),
            pltpu.VMEM((2, pa, LANES), F32),
            pltpu.VMEM((2, pb, LANES), F32),
            pltpu.VMEM((2, 2, depth, LANES), BF16),
            pltpu.VMEM((2, height, half), F32),
            pltpu.VMEM((2, NF, own, half), BF16),
            pltpu.VMEM((2, NF, own, half), BF16),
            pltpu.VMEM((2, NF, own, half), BF16),
            *chain(),
            pltpu.VMEM((NF, 8, LANES), F32),
            pltpu.VMEM((2, 8, LANES), F32),
            pltpu.VMEM((NY, 8, LANES), F32),
            pltpu.VMEM((NZ, 8, LANES), F32),
            pltpu.SemaphoreType.DMA((4,)),
            pltpu.SemaphoreType.DMA((16,)),
            pltpu.SemaphoreType.DMA((192,)),
            pltpu.SemaphoreType.DMA((192,)),
        ],
        compiler_params=pltpu.CompilerParams(
            collective_id=0, has_side_effects=True, vmem_limit_bytes=VMEM_BYTES
        ),
    )(features, labels, probe_weight, sampled)
    return pl.pallas_call(
        write,
        out_shape=(out, out),
        in_specs=[hbm] * 2,
        out_specs=(hbm, hbm),
        scratch_shapes=[
            pltpu.VMEM((2, depth, classes), BF16),
            pltpu.SemaphoreType.DMA((16,)),
            pltpu.SemaphoreType.DMA((16,)),
        ],
        compiler_params=pltpu.CompilerParams(vmem_limit_bytes=VMEM_BYTES),
    )(step, resid)


def solution(mesh):
    in_specs = (P("rows", "feat"), P("rows"), P("feat", None), P("rows"))
    out_specs = (P("feat", None), P("feat", None))
    return jax.shard_map(body, mesh=mesh, in_specs=in_specs, out_specs=out_specs, check_vma=False)
```

```python
import functools

import jax
import jax.numpy as jnp
from jax import lax
from jax.experimental import pallas as pl
from jax.experimental.pallas import tpu as pltpu
from jax.sharding import PartitionSpec as P

MESH = pl.DeviceIdType.MESH
DAMPING = 0.01
F32, BF16 = jnp.float32, jnp.bfloat16
NF, NZ, NY, LANES = 8, 4, 8, 128
FULL = 15.0 - 1.0 / 256.0
VMEM_BYTES = 56 * 1024 * 1024
ORDER_8, ORDER_4 = (4, 3, 5, 2, 6, 1, 7), (2, 1, 3)


def add_all(values):
    return functools.reduce(jnp.add, values)


def total_of(value):
    return jnp.sum(jnp.sum(value, axis=1, keepdims=True), axis=0, keepdims=True)


def kernel(x_hbm, lab_hbm, w_hbm, smp_hbm, step_out, resid_out, step_ref, resid, x_ref, lab_ref, w_ref, smp_ref, xt, part, got_l, err, probs,
           g_keep, g_out, g_in, g_sum, g_ya, g_za, g_zb, g_yb, grad_a, grad_b, grad, pacc, proj, got_p,
           wgt, i_keep, i_out, i_in, i_sum, i_ya, i_za, i_zb, i_yb,
           sc_f, sc_c, sc_y, sc_z, loads, stores, sends, recvs):
    rows = lax.axis_index("rows")
    feat = lax.axis_index("feat")
    core = lax.rem(rows, 2)
    y = lax.rem(rows // 2, NY)
    z = rows // (2 * NY)
    height, depth = x_ref.shape
    own = height // NF
    half = w_ref.shape[1] // 2
    tiles = own // 16 * 4
    top = depth * 2 // 3
    pa, pb = top // NY, (depth - top) // NZ
    total_rows = height * NF * 8
    total_samples = smp_ref.shape[1] * NF * 8

    loaded = [pltpu.make_async_copy(src, dst, loads.at[i]) for i, (src, dst) in enumerate(
        ((x_hbm, x_ref), (w_hbm, w_ref), (lab_hbm, lab_ref), (smp_hbm, smp_ref)))]
    for copy in loaded:
        copy.start()

    def to_feat(k):
        return {"rows": rows, "feat": lax.rem(feat + k, NF)}

    def to_y(k):
        return {"rows": (z * NY + lax.rem(y + k, NY)) * 2 + core, "feat": feat}

    def to_z(k):
        return {"rows": (lax.rem(z + k, NZ) * NY + y) * 2 + core, "feat": feat}

    partner = {"rows": rows + 1 - 2 * core, "feat": feat}
    pending = []

    def send(src, dst, where):
        index = len(pending)
        copy = pltpu.make_async_remote_copy(
            src_ref=src, dst_ref=dst, send_sem=sends.at[index], recv_sem=recvs.at[index], device_id=where,
            device_id_type=MESH,
        )
        copy.start()
        pending.append(copy)
        return copy

    def arrive(copies):
        for copy in copies:
            copy.wait_recv()

    barrier = pltpu.get_barrier_semaphore()
    peers = [partner] + [to_feat(k) for k in ORDER_8] + [to_y(k) for k in ORDER_8] + [to_z(k) for k in ORDER_4]
    for where in peers:
        pl.semaphore_signal(barrier, inc=1, device_id=where, device_id_type=MESH)

    loaded[0].wait()
    loaded[1].wait()
    value = jnp.dot(x_ref[...], w_ref[...], preferred_element_type=F32)
    largest = jnp.maximum(jnp.max(jnp.abs(value), axis=1, keepdims=True), 1e-30)
    power = jnp.ceil(jnp.log2(largest) * 16.0)
    codes = jnp.round(value * jnp.exp2(FULL - power / 16.0)).astype(jnp.int32).astype(jnp.int16)
    powers = jnp.broadcast_to(power, (height, LANES)).astype(jnp.int32).astype(jnp.int16)
    for i in range(NF):
        for r in range(own // 16):
            for c in range(4):
                part[i, 4 * r + c] = codes[i * own + 16 * r:i * own + 16 * (r + 1), c * LANES:(c + 1) * LANES]
            part[i, tiles + r] = powers[i * own + 16 * r:i * own + 16 * (r + 1)]
    pl.semaphore_wait(barrier, len(peers))
    copies = [send(part.at[lax.rem(feat + k, NF)], got_l.at[feat], to_feat(k)) for k in ORDER_8]
    xt[...] = x_ref[...].T
    loaded[2].wait()
    loaded[3].wait()
    row_id = feat * own + lax.broadcasted_iota(jnp.int32, (own, height), 0)
    here = row_id == lax.broadcasted_iota(jnp.int32, (own, height), 1)
    label = jnp.sum(jnp.where(here, lab_ref[...], 0), axis=1, keepdims=True)
    sample_id = feat * own + lax.broadcasted_iota(jnp.int32, (own, smp_ref.shape[1]), 0)
    count = jnp.sum(jnp.where(sample_id == smp_ref[...], 1.0, 0.0), axis=1, keepdims=True)
    got_l[feat] = part[feat]
    arrive(copies)
    pieces = range(own // 16)
    units = [[jnp.exp2(got_l[k, tiles + r].astype(jnp.int32).astype(F32) / 16.0 - FULL) for r in pieces] for k in range(NF)]
    blocks = []
    for c in range(4):
        blocks.append(jnp.concatenate([
            add_all([got_l[k, 4 * r + c].astype(jnp.int32).astype(F32) * units[k][r] for k in range(NF)])
            for r in pieces], axis=0))
    logits = [jnp.concatenate(blocks[2 * side:2 * side + 2], axis=1) for side in range(2)]
    highest = jnp.max(jnp.maximum(*logits), axis=1, keepdims=True)
    expo = [jnp.exp(value - highest) for value in logits]
    bottom = jnp.sum(expo[0] + expo[1], axis=1, keepdims=True)
    for side in range(2):
        p = expo[side] / bottom
        probs[side] = p
        class_id = side * half + lax.broadcasted_iota(jnp.int32, p.shape, 1)
        err[side, feat] = ((p - jnp.where(label == class_id, 1.0, 0.0)) / total_rows).astype(BF16)
    arrive([send(err.at[:, feat], err.at[:, feat], to_feat(k)) for k in ORDER_8])

    def rows_at(start, size):
        return pl.ds(pl.multiple_of(start, size), size)

    a_rows = rows_at(y * pa, pa)
    b_rows = rows_at(top + z * pb, pb)
    both, upper, lower = pl.ds(0, 2), pl.ds(0, top), pl.ds(top, depth - top)

    def sum_rows(mat, full, finish, keep, out, into, total, ya, za, zb, yb, ride):
        def times(side, start, stop):
            return jnp.dot(xt[start:stop], mat[side].reshape(height, half), preferred_element_type=F32)

        value = times(1 - core, 0, top).astype(BF16)
        core_a = []
        for j in range(2):
            out[j, :top] = value[:, j * LANES:(j + 1) * LANES]
            core_a.append([send(out.at[j, upper], into.at[j, upper], partner)])
        value = times(1 - core, top, depth).astype(BF16)
        for j in range(2):
            out[j, top:] = value[:, j * LANES:(j + 1) * LANES]
        core_b = [send(out.at[both, lower], into.at[both, lower], partner)]
        extra = ride(0, None)
        for start, stop in ((0, top), (top, depth)):
            value = times(core, start, stop)
            for j in range(2):
                keep[j, start:stop] = value[:, j * LANES:(j + 1) * LANES]
        extra = ride(1, extra)

        to_ya = []
        for j in range(2):
            arrive(core_a[j])
            total[j, :top] = (keep[j, :top] + into[j, :top].astype(F32)).astype(BF16)
            to_ya.append([send(total.at[j, rows_at(lax.rem(y + k, NY) * pa, pa)], ya.at[j, y], to_y(k)) for k in ORDER_8])
        arrive(core_b)
        for j in range(2):
            total[j, top:] = (keep[j, top:] + into[j, top:].astype(F32)).astype(BF16)
        to_zb = []
        for k in ORDER_4:
            there = rows_at(top + lax.rem(z + k, NZ) * pb, pb)
            to_zb.append(send(total.at[both, there], zb.at[z], to_z(k)))
        zb[z] = total[both, b_rows]
        for j in range(2):
            ya[j, y] = total[j, a_rows]

        arrive(to_zb)
        yb[y] = add_all([zb[k].astype(F32) for k in range(NZ)]).astype(BF16)
        to_yb = [send(yb.at[y], yb.at[y], to_y(k)) for k in ORDER_8]
        to_za = []
        for j in range(2):
            arrive(to_ya[j])
            za[j, z] = add_all([ya[j, k].astype(F32) for k in range(NY)]).astype(BF16)
            to_za.append([send(za.at[j, z], za.at[j, z], to_z(k)) for k in ORDER_4])
            if j == 0:
                extra = ride(2, extra)

        ride(3, extra)
        from_ya = []

        def gather_a(j):
            arrive(to_za[j])
            mine = full.at[core, j, a_rows]
            mine[...] = finish(j, add_all([za[j, k].astype(F32) for k in range(NZ)])).astype(BF16)
            from_ya.append([send(mine, mine, to_y(k)) for k in ORDER_8])

        gather_a(0)
        arrive(to_yb)
        mine = full.at[core, both, b_rows]
        mine[...] = finish(2, add_all([yb[k].astype(F32) for k in range(NY)])).astype(BF16)
        from_zb = [send(mine, mine, to_z(k)) for k in ORDER_4]
        gather_a(1)
        across = []
        for j in range(2):
            arrive(from_ya[j])
            mine = full.at[core, j, upper]
            across.append([send(mine, mine, partner)])
            yield core, j, across[j]
        for j in range(2):
            arrive(across[j])
        yield 1 - core, 0, None
        arrive(from_zb)
        mine = full.at[core, both, lower]
        across = [send(mine, mine, partner)]
        yield core, 2, None
        arrive(across)
        yield 1 - core, 2, None

    norms = []

    def damped(part, value):
        if part < 2:
            lane = pl.multiple_of(core * half + part * LANES, LANES)
            value = value + DAMPING * w_ref[a_rows, pl.ds(lane, LANES)].astype(F32)
            grad_a[part] = value
            norms.append(total_of(value * value) / NZ)
        else:
            lane = pl.multiple_of(core * half, half)
            weight = w_ref[b_rows, pl.ds(lane, half)].astype(F32)
            value = value + DAMPING * jnp.stack([weight[:, :LANES], weight[:, LANES:]])
            grad_b[...] = value
            norms.append(total_of(value[0] * value[0] + value[1] * value[1]) / NY)
        return value

    arrivals = []
    for side, part, _ in sum_rows(
            err, grad, damped, g_keep, g_out, g_in, g_sum, g_ya, g_za, g_zb, g_yb, lambda *_: None):
        here = slice(0, top) if part < 2 else slice(top, depth)
        if part == 0 and _ is not None:
            continue
        mat = jnp.concatenate([grad[side, 0, here], grad[side, 1, here]], axis=1)
        value = jnp.dot(x_ref[:, here], mat, preferred_element_type=F32)
        if part < 2:
            pacc[side] = value
        else:
            proj[side] = (pacc[side] + value).astype(BF16).reshape(proj.shape[1:])
            arrivals += [send(proj.at[side, lax.rem(feat + k, NF)], got_p.at[side, feat], to_feat(k)) for k in ORDER_8]
    norm = add_all(norms)
    for side in range(2):
        got_p[side, feat] = proj[side, feat]
    arrive(arrivals)
    quarters = [(side, j) for side in range(2) for j in range(2)]
    pj = [add_all([got_p[side, k, :, j * LANES:(j + 1) * LANES].astype(F32) for k in range(NF)]) for side, j in quarters]
    ps = [probs[side, :, j * LANES:(j + 1) * LANES] for side, j in quarters]
    pp = [a * b for a, b in zip(ps, pj)]
    inner = jnp.sum(add_all(pp), axis=1, keepdims=True)
    scale = count / total_samples
    weighted = [((a - b * inner) * scale).astype(BF16) for a, b in zip(pp, ps)]
    for (side, j), value in zip(quarters, weighted):
        wgt[side, feat, :, j * LANES:(j + 1) * LANES] = value
    copies = [send(wgt.at[:, feat], wgt.at[:, feat], to_feat(k)) for k in ORDER_8]
    curv = total_of(add_all([a.astype(F32) * b for a, b in zip(weighted, pj)]))
    upper_half = lax.broadcasted_iota(jnp.int32, (8, LANES), 0) < 4
    sc_f[feat] = jnp.where(upper_half, norm, curv)
    scalars = [send(sc_f.at[feat], sc_f.at[feat], to_feat(k)) for k in ORDER_8]
    arrive(copies)

    alpha = []

    def ride(stage, copies):
        if stage == 0:
            arrive(scalars)
            sc_c[core] = add_all([sc_f[k] for k in range(NF)])
            return [send(sc_c.at[core], sc_c.at[core], partner)]
        arrive(copies)
        if stage == 1:
            sc_y[y] = sc_c[0] + sc_c[1]
            return [send(sc_y.at[y], sc_y.at[y], to_y(k)) for k in ORDER_8]
        if stage == 2:
            sc_z[z] = add_all([sc_y[k] for k in range(NY)])
            return [send(sc_z.at[z], sc_z.at[z], to_z(k)) for k in ORDER_4]
        sums = add_all([sc_z[k] for k in range(NZ)])
        alpha.append(sums[0:1, 0:1] / (sums[4:5, 0:1] + DAMPING * sums[0:1, 0:1]))
        return None

    def residual(part, value):
        g = grad_a[part] if part < 2 else grad_b[...]
        return -g + alpha[0] * (value + DAMPING * g)

    stored = []

    def store(src, dst, side, j, here):
        lanes = pl.ds(pl.multiple_of((2 * side + j) * LANES, LANES), LANES)
        copy = pltpu.make_async_copy(src.at[side, j, here], dst.at[here, lanes], stores.at[len(stored)])
        copy.start()
        stored.append(copy)

    first = True
    for side, part, _ in sum_rows(
            wgt, resid, residual, i_keep, i_out, i_in, i_sum, i_ya, i_za, i_zb, i_yb, ride):
        if first:
            first = False
            for one, j in quarters:
                step_ref[one, j] = (-alpha[0] * grad[one, j].astype(F32)).astype(BF16)
                store(step_ref, step_out, one, j, pl.ds(0, depth))
        if part == 2:
            for j in range(2):
                store(resid, resid_out, side, j, lower)
        elif _ is not None:
            store(resid, resid_out, side, part, upper)
        else:
            for j in range(2):
                store(resid, resid_out, side, j, upper)
    for copy in stored:
        copy.wait()
    for copy in pending:
        copy.wait_send()


def write(step_ref, resid_ref, step_out, resid_out, held, ins, outs):
    depth = step_ref.shape[0]
    loads, stores = [], []
    for n, (src, dst) in enumerate(((step_ref, step_out), (resid_ref, resid_out))):
        for part in range(4):
            some = pl.ds(part * (depth // 4), depth // 4)
            index = len(loads)
            loads.append(pltpu.make_async_copy(src.at[some], held.at[n, some], ins.at[index]))
            stores.append(pltpu.make_async_copy(held.at[n, some], dst.at[some], outs.at[index]))
    for copy in loads:
        copy.start()
    for there, back in zip(loads, stores):
        there.wait()
        back.start()
    for copy in stores:
        copy.wait()


def body(features, labels, probe_weight, sampled):
    height, depth = features.shape
    classes = probe_weight.shape[1]
    half = classes // 2
    own = height // NF
    top = depth * 2 // 3
    pa, pb = top // NY, (depth - top) // NZ
    hbm = pl.BlockSpec(memory_space=pltpu.HBM)
    out = jax.ShapeDtypeStruct((depth, classes), BF16)
    labels = labels.reshape(1, height)
    sampled = sampled.reshape(1, sampled.shape[0])

    def chain():
        return [
            pltpu.VMEM((2, depth, LANES), F32),
            pltpu.VMEM((2, depth, LANES), BF16),
            pltpu.VMEM((2, depth, LANES), BF16),
            pltpu.VMEM((2, depth, LANES), BF16),
            pltpu.VMEM((2, NY, pa, LANES), BF16),
            pltpu.VMEM((2, NZ, pa, LANES), BF16),
            pltpu.VMEM((NZ, 2, pb, LANES), BF16),
            pltpu.VMEM((NY, 2, pb, LANES), BF16),
        ]

    step, resid = pl.pallas_call(
        kernel,
        out_shape=(out, out),
        in_specs=[hbm] * 4,
        out_specs=(hbm, hbm),
        scratch_shapes=[
            pltpu.VMEM((2, 2, depth, LANES), BF16),
            pltpu.VMEM((2, 2, depth, LANES), BF16),
            pltpu.VMEM(features.shape, BF16),
            pltpu.VMEM(labels.shape, jnp.int32),
            pltpu.VMEM(probe_weight.shape, BF16),
            pltpu.VMEM(sampled.shape, jnp.int32),
            pltpu.VMEM((depth, height), BF16),
            pltpu.VMEM((NF, own // 16 * 5, 16, LANES), jnp.int16),
            pltpu.VMEM((NF, own // 16 * 5, 16, LANES), jnp.int16),
            pltpu.VMEM((2, NF, own, half), BF16),
            pltpu.VMEM((2, own, half), F32),
            *chain(),
            pltpu.VMEM((2, pa, LANES), F32),
            pltpu.VMEM((2, pb, LANES), F32),
            pltpu.VMEM((2, 2, depth, LANES), BF16),
            pltpu.VMEM((2, height, half), F32),
            pltpu.VMEM((2, NF, own, half), BF16),
            pltpu.VMEM((2, NF, own, half), BF16),
            pltpu.VMEM((2, NF, own, half), BF16),
            *chain(),
            pltpu.VMEM((NF, 8, LANES), F32),
            pltpu.VMEM((2, 8, LANES), F32),
            pltpu.VMEM((NY, 8, LANES), F32),
            pltpu.VMEM((NZ, 8, LANES), F32),
            pltpu.SemaphoreType.DMA((4,)),
            pltpu.SemaphoreType.DMA((16,)),
            pltpu.SemaphoreType.DMA((192,)),
            pltpu.SemaphoreType.DMA((192,)),
        ],
        compiler_params=pltpu.CompilerParams(
            collective_id=0, has_side_effects=True, vmem_limit_bytes=VMEM_BYTES
        ),
    )(features, labels, probe_weight, sampled)
    return pl.pallas_call(
        write,
        out_shape=(out, out),
        in_specs=[hbm] * 2,
        out_specs=(hbm, hbm),
        scratch_shapes=[
            pltpu.VMEM((2, depth, classes), BF16),
            pltpu.SemaphoreType.DMA((16,)),
            pltpu.SemaphoreType.DMA((16,)),
        ],
        compiler_params=pltpu.CompilerParams(vmem_limit_bytes=VMEM_BYTES),
    )(step, resid)


def solution(mesh):
    in_specs = (P("rows", "feat"), P("rows"), P("feat", None), P("rows"))
    out_specs = (P("feat", None), P("feat", None))
    return jax.shard_map(body, mesh=mesh, in_specs=in_specs, out_specs=out_specs, check_vma=False)
```

```python
import functools

import jax
import jax.numpy as jnp
from jax import lax
from jax.experimental import pallas as pl
from jax.experimental.pallas import tpu as pltpu
from jax.sharding import PartitionSpec as P

MESH = pl.DeviceIdType.MESH
DAMPING = 0.01
F32, BF16 = jnp.float32, jnp.bfloat16
NF, NZ, NY, LANES = 8, 4, 8, 128
FULL = 15.0 - 1.0 / 256.0
VMEM_BYTES = 56 * 1024 * 1024
ORDER_8, ORDER_4 = (4, 3, 5, 2, 6, 1, 7), (2, 1, 3)


def add_all(values):
    return functools.reduce(jnp.add, values)


def total_of(value):
    return jnp.sum(jnp.sum(value, axis=1, keepdims=True), axis=0, keepdims=True)


def kernel(x_hbm, lab_hbm, w_hbm, smp_hbm, step_out, resid_out, step_ref, resid, x_ref, lab_ref, w_ref, smp_ref, x_other, xt, part, got_l, err_out, err, probs,
           g_sum, g_ya, g_za, g_zb, g_yb, grad_a, grad_b, grad, pacc, proj, got_p,
           wgt_out, wgt, i_sum, i_ya, i_za, i_zb, i_yb,
           sc_own, sc_f, sc_y, sc_z, loads, stores, sends, recvs):
    rows = lax.axis_index("rows")
    feat = lax.axis_index("feat")
    core = lax.rem(rows, 2)
    y = lax.rem(rows // 2, NY)
    z = rows // (2 * NY)
    height, depth = x_ref.shape
    own = height // NF
    half = w_ref.shape[1] // 2
    tiles = own // 16 * 4
    top = depth * 2 // 3
    pa, pb = top // NY, (depth - top) // NZ
    total_rows = height * NF * 8
    total_samples = smp_ref.shape[1] * NF * 8

    loaded = [pltpu.make_async_copy(src, dst, loads.at[i]) for i, (src, dst) in enumerate(
        ((x_hbm, x_ref), (w_hbm, w_ref), (lab_hbm, lab_ref), (smp_hbm, smp_ref)))]
    for copy in loaded:
        copy.start()

    def to_feat(k):
        return {"rows": rows, "feat": lax.rem(feat + k, NF)}

    def to_y(k):
        return {"rows": (z * NY + lax.rem(y + k, NY)) * 2 + core, "feat": feat}

    def to_z(k):
        return {"rows": (lax.rem(z + k, NZ) * NY + y) * 2 + core, "feat": feat}

    partner = {"rows": rows + 1 - 2 * core, "feat": feat}

    def to_other(k):
        return {"rows": rows + 1 - 2 * core, "feat": lax.rem(feat + k, NF)}

    pending = []

    def send(src, dst, where):
        index = len(pending)
        copy = pltpu.make_async_remote_copy(
            src_ref=src, dst_ref=dst, send_sem=sends.at[index], recv_sem=recvs.at[index], device_id=where,
            device_id_type=MESH,
        )
        copy.start()
        pending.append(copy)
        return copy

    def arrive(copies):
        for copy in copies:
            copy.wait_recv()

    barrier = pltpu.get_barrier_semaphore()
    peers = [to_y(4), to_z(2)] + [to_y(k) for k in (3, 5)] + [to_feat(k) for k in (3, 5, 4)]
    peers += [to_other(k) for k in ORDER_8] + [to_z(1), to_z(3), to_y(2), to_y(6)] + [to_feat(k) for k in (2, 6, 1, 7)] + [to_y(1), to_y(7), partner]
    for where in peers:
        pl.semaphore_signal(barrier, inc=1, device_id=where, device_id_type=MESH)

    loaded[0].wait()
    loaded[1].wait()
    value = jnp.dot(x_ref[...], w_ref[...], preferred_element_type=F32)
    largest = jnp.maximum(jnp.max(jnp.abs(value), axis=1, keepdims=True), 1e-30)
    power = jnp.ceil(jnp.log2(largest) * 16.0)
    codes = jnp.round(value * jnp.exp2(FULL - power / 16.0)).astype(jnp.int32).astype(jnp.int16)
    powers = jnp.broadcast_to(power, (height, LANES)).astype(jnp.int32).astype(jnp.int16)
    for i in range(NF):
        for r in range(own // 16):
            for c in range(4):
                part[i, 4 * r + c] = codes[i * own + 16 * r:i * own + 16 * (r + 1), c * LANES:(c + 1) * LANES]
            part[i, tiles + r] = powers[i * own + 16 * r:i * own + 16 * (r + 1)]
    pl.semaphore_wait(barrier, len(peers))
    copies = [send(part.at[lax.rem(feat + k, NF)], got_l.at[feat], to_feat(k)) for k in ORDER_8]
    copy_x = send(x_ref, x_other, partner)
    xt[:, :height] = x_ref[...].T
    loaded[2].wait()
    loaded[3].wait()
    row_id = feat * own + lax.broadcasted_iota(jnp.int32, (own, height), 0)
    here = row_id == lax.broadcasted_iota(jnp.int32, (own, height), 1)
    label = jnp.sum(jnp.where(here, lab_ref[...], 0), axis=1, keepdims=True)
    sample_id = feat * own + lax.broadcasted_iota(jnp.int32, (own, smp_ref.shape[1]), 0)
    count = jnp.sum(jnp.where(sample_id == smp_ref[...], 1.0, 0.0), axis=1, keepdims=True)
    got_l[feat] = part[feat]
    arrive([copy_x])
    xt[:, height:] = x_other[...].T
    arrive(copies)
    pieces = range(own // 16)
    units = [[jnp.exp2(got_l[k, tiles + r].astype(jnp.int32).astype(F32) / 16.0 - FULL) for r in pieces] for k in range(NF)]
    blocks = []
    for c in range(4):
        blocks.append(jnp.concatenate([
            add_all([got_l[k, 4 * r + c].astype(jnp.int32).astype(F32) * units[k][r] for k in range(NF)])
            for r in pieces], axis=0))
    logits = [jnp.concatenate(blocks[2 * side:2 * side + 2], axis=1) for side in range(2)]
    highest = jnp.max(jnp.maximum(*logits), axis=1, keepdims=True)
    expo = [jnp.exp(value - highest) for value in logits]
    bottom = jnp.sum(expo[0] + expo[1], axis=1, keepdims=True)
    for side in range(2):
        p = expo[side] / bottom
        probs[side] = p
        class_id = side * half + lax.broadcasted_iota(jnp.int32, p.shape, 1)
        err_out[lax.rem(core + side, 2)] = ((p - jnp.where(label == class_id, 1.0, 0.0)) / total_rows).astype(BF16)

    def to_chips(out, into):
        copies = [send(out.at[1], into.at[1, feat], partner)]
        for k in ORDER_8:
            copies.append(send(out.at[0], into.at[0, feat], to_feat(k)))
            copies.append(send(out.at[1], into.at[1, feat], to_other(k)))
        into[0, feat] = out[0]
        return copies

    arrive(to_chips(err_out, err))

    def rows_at(start, size):
        return pl.ds(pl.multiple_of(start, size), size)

    a_rows = rows_at(y * pa, pa)
    b_rows = rows_at(top + z * pb, pb)
    both, upper, lower = pl.ds(0, 2), pl.ds(0, top), pl.ds(top, depth - top)

    def sum_rows(mat, full, finish, total, ya, za, zb, yb, ride):
        def times(start, stop):
            value = jnp.dot(xt[start:stop], mat[...].reshape(2 * height, half), preferred_element_type=F32).astype(BF16)
            for j in range(2):
                total[j, start:stop] = value[:, j * LANES:(j + 1) * LANES]

        times(0, top)
        extra = ride(1, None)
        to_ya = []
        for j in range(2):
            to_ya.append([send(total.at[j, rows_at(lax.rem(y + k, NY) * pa, pa)], ya.at[j, y], to_y(k)) for k in ORDER_8])
        times(top, depth)
        to_zb = []
        for k in ORDER_4:
            there = rows_at(top + lax.rem(z + k, NZ) * pb, pb)
            to_zb.append(send(total.at[both, there], zb.at[z], to_z(k)))
        zb[z] = total[both, b_rows]
        for j in range(2):
            ya[j, y] = total[j, a_rows]

        arrive(to_zb)
        yb[y] = add_all([zb[k].astype(F32) for k in range(NZ)]).astype(BF16)
        to_yb = [send(yb.at[y], yb.at[y], to_y(k)) for k in ORDER_8]
        to_za = []
        for j in range(2):
            arrive(to_ya[j])
            za[j, z] = add_all([ya[j, k].astype(F32) for k in range(NY)]).astype(BF16)
            to_za.append([send(za.at[j, z], za.at[j, z], to_z(k)) for k in ORDER_4])
            if j == 0:
                extra = ride(2, extra)

        ride(3, extra)
        from_ya = []

        def gather_a(j):
            arrive(to_za[j])
            mine = full.at[core, j, a_rows]
            mine[...] = finish(j, add_all([za[j, k].astype(F32) for k in range(NZ)])).astype(BF16)
            from_ya.append([send(mine, mine, to_y(k)) for k in ORDER_8])

        gather_a(0)
        arrive(to_yb)
        mine = full.at[core, both, b_rows]
        mine[...] = finish(2, add_all([yb[k].astype(F32) for k in range(NY)])).astype(BF16)
        from_zb = [send(mine, mine, to_z(k)) for k in ORDER_4]
        gather_a(1)
        ride(4, None)
        across = []
        for j in range(2):
            arrive(from_ya[j])
            mine = full.at[core, j, upper]
            across.append([send(mine, mine, partner)])
            yield core, j, across[j]
        for j in range(2):
            arrive(across[j])
        yield 1 - core, 0, None
        arrive(from_zb)
        mine = full.at[core, both, lower]
        across = [send(mine, mine, partner)]
        yield core, 2, None
        arrive(across)
        yield 1 - core, 2, None

    norms = []

    def damped(part, value):
        if part < 2:
            lane = pl.multiple_of(core * half + part * LANES, LANES)
            value = value + DAMPING * w_ref[a_rows, pl.ds(lane, LANES)].astype(F32)
            grad_a[part] = value
            norms.append(total_of(value * value) / NZ)
        else:
            lane = pl.multiple_of(core * half, half)
            weight = w_ref[b_rows, pl.ds(lane, half)].astype(F32)
            value = value + DAMPING * jnp.stack([weight[:, :LANES], weight[:, LANES:]])
            grad_b[...] = value
            norms.append(total_of(value[0] * value[0] + value[1] * value[1]) / NY)
        return value

    arrivals = []
    for side, part, _ in sum_rows(
            err, grad, damped, g_sum, g_ya, g_za, g_zb, g_yb, lambda *_: None):
        here = slice(0, top) if part < 2 else slice(top, depth)
        if part == 0 and _ is not None:
            continue
        mat = jnp.concatenate([grad[side, 0, here], grad[side, 1, here]], axis=1)
        value = jnp.dot(x_ref[:, here], mat, preferred_element_type=F32)
        if part < 2:
            pacc[side] = value
        else:
            proj[side] = (pacc[side] + value).astype(BF16).reshape(proj.shape[1:])
            arrivals += [send(proj.at[side, lax.rem(feat + k, NF)], got_p.at[side, feat], to_feat(k)) for k in ORDER_8]
    norm = add_all(norms)
    for side in range(2):
        got_p[side, feat] = proj[side, feat]
    arrive(arrivals)
    quarters = [(side, j) for side in range(2) for j in range(2)]
    pj = [add_all([got_p[side, k, :, j * LANES:(j + 1) * LANES].astype(F32) for k in range(NF)]) for side, j in quarters]
    ps = [probs[side, :, j * LANES:(j + 1) * LANES] for side, j in quarters]
    pp = [a * b for a, b in zip(ps, pj)]
    inner = jnp.sum(add_all(pp), axis=1, keepdims=True)
    scale = count / total_samples
    weighted = [((a - b * inner) * scale).astype(BF16) for a, b in zip(pp, ps)]
    for (side, j), value in zip(quarters, weighted):
        wgt_out[lax.rem(core + side, 2), :, j * LANES:(j + 1) * LANES] = value
    copies = to_chips(wgt_out, wgt)
    curv = total_of(add_all([a.astype(F32) * b for a, b in zip(weighted, pj)]))
    upper_half = lax.broadcasted_iota(jnp.int32, (8, LANES), 0) < 4
    sc_own[...] = jnp.where(upper_half, norm, curv)
    scalars = [send(sc_own, sc_f.at[1, feat], partner)]
    for k in ORDER_8:
        scalars.append(send(sc_own, sc_f.at[0, feat], to_feat(k)))
        scalars.append(send(sc_own, sc_f.at[1, feat], to_other(k)))
    sc_f[0, feat] = sc_own[...]
    arrive(copies)

    alpha = []

    def ride(stage, copies):
        if stage == 1:
            arrive(scalars)
            both_cores = [add_all([sc_f[lax.rem(core + one, 2), k] for k in range(NF)]) for one in range(2)]
            sc_y[y] = both_cores[0] + both_cores[1]
            return [send(sc_y.at[y], sc_y.at[y], to_y(k)) for k in ORDER_8]
        if copies:
            arrive(copies)
        if stage == 2:
            sc_z[z] = add_all([sc_y[k] for k in range(NY)])
            return [send(sc_z.at[z], sc_z.at[z], to_z(k)) for k in ORDER_4]
        if stage == 3:
            sums = add_all([sc_z[k] for k in range(NZ)])
            alpha.append(sums[0:1, 0:1] / (sums[4:5, 0:1] + DAMPING * sums[0:1, 0:1]))
        else:
            for side, j in quarters:
                step_ref[side, j] = (-alpha[0] * grad[side, j].astype(F32)).astype(BF16)
                store(step_ref, step_out, side, j, pl.ds(0, depth))
        return None

    def residual(part, value):
        g = grad_a[part] if part < 2 else grad_b[...]
        return -g + alpha[0] * (value + DAMPING * g)

    stored = []

    def store(src, dst, side, j, here):
        lanes = pl.ds(pl.multiple_of((2 * side + j) * LANES, LANES), LANES)
        copy = pltpu.make_async_copy(src.at[side, j, here], dst.at[here, lanes], stores.at[len(stored)])
        copy.start()
        stored.append(copy)

    for side, part, _ in sum_rows(
            wgt, resid, residual, i_sum, i_ya, i_za, i_zb, i_yb, ride):
        if part == 2:
            for j in range(2):
                store(resid, resid_out, side, j, lower)
        elif _ is not None:
            store(resid, resid_out, side, part, upper)
        else:
            for j in range(2):
                store(resid, resid_out, side, j, upper)
    for copy in stored:
        copy.wait()
    for copy in pending:
        copy.wait_send()


def write(step_ref, resid_ref, step_out, resid_out, held, ins, outs):
    depth = step_ref.shape[0]
    loads, stores = [], []
    for n, (src, dst) in enumerate(((step_ref, step_out), (resid_ref, resid_out))):
        for part in range(4):
            some = pl.ds(part * (depth // 4), depth // 4)
            index = len(loads)
            loads.append(pltpu.make_async_copy(src.at[some], held.at[n, some], ins.at[index]))
            stores.append(pltpu.make_async_copy(held.at[n, some], dst.at[some], outs.at[index]))
    for copy in loads:
        copy.start()
    for there, back in zip(loads, stores):
        there.wait()
        back.start()
    for copy in stores:
        copy.wait()


def body(features, labels, probe_weight, sampled):
    height, depth = features.shape
    classes = probe_weight.shape[1]
    half = classes // 2
    own = height // NF
    top = depth * 2 // 3
    pa, pb = top // NY, (depth - top) // NZ
    hbm = pl.BlockSpec(memory_space=pltpu.HBM)
    out = jax.ShapeDtypeStruct((depth, classes), BF16)
    labels = labels.reshape(1, height)
    sampled = sampled.reshape(1, sampled.shape[0])

    def chain():
        return [
            pltpu.VMEM((2, depth, LANES), BF16),
            pltpu.VMEM((2, NY, pa, LANES), BF16),
            pltpu.VMEM((2, NZ, pa, LANES), BF16),
            pltpu.VMEM((NZ, 2, pb, LANES), BF16),
            pltpu.VMEM((NY, 2, pb, LANES), BF16),
        ]

    step, resid = pl.pallas_call(
        kernel,
        out_shape=(out, out),
        in_specs=[hbm] * 4,
        out_specs=(hbm, hbm),
        scratch_shapes=[
            pltpu.VMEM((2, 2, depth, LANES), BF16),
            pltpu.VMEM((2, 2, depth, LANES), BF16),
            pltpu.VMEM(features.shape, BF16),
            pltpu.VMEM(labels.shape, jnp.int32),
            pltpu.VMEM(probe_weight.shape, BF16),
            pltpu.VMEM(sampled.shape, jnp.int32),
            pltpu.VMEM(features.shape, BF16),
            pltpu.VMEM((depth, 2 * height), BF16),
            pltpu.VMEM((NF, own // 16 * 5, 16, LANES), jnp.int16),
            pltpu.VMEM((NF, own // 16 * 5, 16, LANES), jnp.int16),
            pltpu.VMEM((2, own, half), BF16),
            pltpu.VMEM((2, NF, own, half), BF16),
            pltpu.VMEM((2, own, half), F32),
            *chain(),
            pltpu.VMEM((2, pa, LANES), F32),
            pltpu.VMEM((2, pb, LANES), F32),
            pltpu.VMEM((2, 2, depth, LANES), BF16),
            pltpu.VMEM((2, height, half), F32),
            pltpu.VMEM((2, NF, own, half), BF16),
            pltpu.VMEM((2, NF, own, half), BF16),
            pltpu.VMEM((2, own, half), BF16),
            pltpu.VMEM((2, NF, own, half), BF16),
            *chain(),
            pltpu.VMEM((8, LANES), F32),
            pltpu.VMEM((2, NF, 8, LANES), F32),
            pltpu.VMEM((NY, 8, LANES), F32),
            pltpu.VMEM((NZ, 8, LANES), F32),
            pltpu.SemaphoreType.DMA((4,)),
            pltpu.SemaphoreType.DMA((16,)),
            pltpu.SemaphoreType.DMA((208,)),
            pltpu.SemaphoreType.DMA((208,)),
        ],
        compiler_params=pltpu.CompilerParams(
            collective_id=0, has_side_effects=True, vmem_limit_bytes=VMEM_BYTES
        ),
    )(features, labels, probe_weight, sampled)
    return pl.pallas_call(
        write,
        out_shape=(out, out),
        in_specs=[hbm] * 2,
        out_specs=(hbm, hbm),
        scratch_shapes=[
            pltpu.VMEM((2, depth, classes), BF16),
            pltpu.SemaphoreType.DMA((16,)),
            pltpu.SemaphoreType.DMA((16,)),
        ],
        compiler_params=pltpu.CompilerParams(vmem_limit_bytes=VMEM_BYTES),
    )(step, resid)


def solution(mesh):
    in_specs = (P("rows", "feat"), P("rows"), P("feat", None), P("rows"))
    out_specs = (P("feat", None), P("feat", None))
    return jax.shard_map(body, mesh=mesh, in_specs=in_specs, out_specs=out_specs, check_vma=False)
```

```python
import functools

import jax
import jax.numpy as jnp
from jax import lax
from jax.experimental import pallas as pl
from jax.experimental.pallas import tpu as pltpu
from jax.sharding import PartitionSpec as P

MESH = pl.DeviceIdType.MESH
DAMPING = 0.01
F32, BF16 = jnp.float32, jnp.bfloat16
NF, NZ, NY, LANES = 8, 4, 8, 128
FULL = 15.0 - 1.0 / 256.0
VMEM_BYTES = 56 * 1024 * 1024
ORDER_8, ORDER_4 = (4, 3, 5, 2, 6, 1, 7), (2, 1, 3)


def add_all(values):
    return functools.reduce(jnp.add, values)


def total_of(value):
    return jnp.sum(jnp.sum(value, axis=1, keepdims=True), axis=0, keepdims=True)


def kernel(x_hbm, lab_hbm, w_hbm, smp_hbm, step_out, resid_out, step_ref, resid, x_ref, lab_ref, w_ref, smp_ref, x_other, xt, part, got_l, err_out, err, probs,
           g_sum, g_ya, g_za, g_zb, g_yb, grad_a, grad_b, grad, pacc, proj, got_p,
           wgt_out, wgt, i_sum, i_ya, i_za, i_zb, i_yb,
           sc_own, sc_f, sc_y, sc_z, loads, stores, sends, recvs):
    rows = lax.axis_index("rows")
    feat = lax.axis_index("feat")
    core = lax.rem(rows, 2)
    y = lax.rem(rows // 2, NY)
    z = rows // (2 * NY)
    height, depth = x_ref.shape
    own = height // NF
    half = w_ref.shape[1] // 2
    tiles = own // 16 * 4
    top = depth * 2 // 3
    pa, pb = top // NY, (depth - top) // NZ
    total_rows = height * NF * 8
    total_samples = smp_ref.shape[1] * NF * 8

    loaded = [pltpu.make_async_copy(src, dst, loads.at[i]) for i, (src, dst) in enumerate(
        ((x_hbm, x_ref), (w_hbm, w_ref), (lab_hbm, lab_ref), (smp_hbm, smp_ref)))]
    for copy in loaded:
        copy.start()

    def to_feat(k):
        return {"rows": rows, "feat": lax.rem(feat + k, NF)}

    def to_y(k):
        return {"rows": (z * NY + lax.rem(y + k, NY)) * 2 + core, "feat": feat}

    def to_z(k):
        return {"rows": (lax.rem(z + k, NZ) * NY + y) * 2 + core, "feat": feat}

    partner = {"rows": rows + 1 - 2 * core, "feat": feat}

    def to_other(k):
        return {"rows": rows + 1 - 2 * core, "feat": lax.rem(feat + k, NF)}

    pending = []

    def send(src, dst, where):
        index = len(pending)
        copy = pltpu.make_async_remote_copy(
            src_ref=src, dst_ref=dst, send_sem=sends.at[index], recv_sem=recvs.at[index], device_id=where,
            device_id_type=MESH,
        )
        copy.start()
        pending.append(copy)
        return copy

    def arrive(copies):
        for copy in copies:
            copy.wait_recv()

    barrier = pltpu.get_barrier_semaphore()
    peers = [to_y(4), to_z(2)] + [to_y(k) for k in (3, 5)] + [to_feat(k) for k in (3, 5, 4)]
    peers += [to_other(k) for k in ORDER_8] + [to_z(1), to_z(3), to_y(2), to_y(6)] + [to_feat(k) for k in (2, 6, 1, 7)] + [to_y(1), to_y(7), partner]
    for where in peers:
        pl.semaphore_signal(barrier, inc=1, device_id=where, device_id_type=MESH)

    loaded[0].wait()
    loaded[1].wait()
    value = jnp.dot(x_ref[...], w_ref[...], preferred_element_type=F32)
    largest = jnp.maximum(jnp.max(jnp.abs(value), axis=1, keepdims=True), 1e-30)
    power = jnp.ceil(jnp.log2(largest) * 16.0)
    codes = jnp.round(value * jnp.exp2(FULL - power / 16.0)).astype(jnp.int32).astype(jnp.int16)
    powers = jnp.broadcast_to(power, (height, LANES)).astype(jnp.int32).astype(jnp.int16)
    for i in range(NF):
        for r in range(own // 16):
            for c in range(4):
                part[i, 4 * r + c] = codes[i * own + 16 * r:i * own + 16 * (r + 1), c * LANES:(c + 1) * LANES]
            part[i, tiles + r] = powers[i * own + 16 * r:i * own + 16 * (r + 1)]
    pl.semaphore_wait(barrier, len(peers))
    copies = [send(part.at[lax.rem(feat + k, NF)], got_l.at[feat], to_feat(k)) for k in ORDER_8]
    copy_x = send(x_ref, x_other, partner)
    xt[:, :height] = x_ref[...].T
    loaded[2].wait()
    loaded[3].wait()
    row_id = feat * own + lax.broadcasted_iota(jnp.int32, (own, height), 0)
    here = row_id == lax.broadcasted_iota(jnp.int32, (own, height), 1)
    label = jnp.sum(jnp.where(here, lab_ref[...], 0), axis=1, keepdims=True)
    sample_id = feat * own + lax.broadcasted_iota(jnp.int32, (own, smp_ref.shape[1]), 0)
    count = jnp.sum(jnp.where(sample_id == smp_ref[...], 1.0, 0.0), axis=1, keepdims=True)
    got_l[feat] = part[feat]
    arrive([copy_x])
    xt[:, height:] = x_other[...].T
    arrive(copies)
    pieces = range(own // 16)
    units = [[jnp.exp2(got_l[k, tiles + r].astype(jnp.int32).astype(F32) / 16.0 - FULL) for r in pieces] for k in range(NF)]
    blocks = []
    for c in range(4):
        blocks.append(jnp.concatenate([
            add_all([got_l[k, 4 * r + c].astype(jnp.int32).astype(F32) * units[k][r] for k in range(NF)])
            for r in pieces], axis=0))
    logits = [jnp.concatenate(blocks[2 * side:2 * side + 2], axis=1) for side in range(2)]
    highest = jnp.max(jnp.maximum(*logits), axis=1, keepdims=True)
    expo = [jnp.exp(value - highest) for value in logits]
    bottom = jnp.sum(expo[0] + expo[1], axis=1, keepdims=True)
    for side in range(2):
        p = expo[side] / bottom
        probs[side] = p
        class_id = side * half + lax.broadcasted_iota(jnp.int32, p.shape, 1)
        err_out[lax.rem(core + side, 2)] = ((p - jnp.where(label == class_id, 1.0, 0.0)) / total_rows).astype(BF16)

    def to_chips(out, into):
        copies = [send(out.at[1], into.at[1, feat], partner)]
        for k in ORDER_8:
            copies.append(send(out.at[0], into.at[0, feat], to_feat(k)))
            copies.append(send(out.at[1], into.at[1, feat], to_other(k)))
        into[0, feat] = out[0]
        return copies

    arrive(to_chips(err_out, err))

    def rows_at(start, size):
        return pl.ds(pl.multiple_of(start, size), size)

    a_rows = rows_at(y * pa, pa)
    b_rows = rows_at(top + z * pb, pb)
    both, upper, lower = pl.ds(0, 2), pl.ds(0, top), pl.ds(top, depth - top)

    def sum_rows(mat, full, finish, total, ya, za, zb, yb, ride):
        def times(start, stop):
            value = jnp.dot(xt[start:stop], mat[...].reshape(2 * height, half), preferred_element_type=F32).astype(BF16)
            for j in range(2):
                total[j, start:stop] = value[:, j * LANES:(j + 1) * LANES]

        times(0, top)
        to_ya = []
        for j in range(2):
            to_ya.append([send(total.at[j, rows_at(lax.rem(y + k, NY) * pa, pa)], ya.at[j, y], to_y(k)) for k in ORDER_8])
            if j == 0:
                extra = ride(1, None)
        times(top, depth)
        to_zb = []
        for k in ORDER_4:
            there = rows_at(top + lax.rem(z + k, NZ) * pb, pb)
            to_zb.append(send(total.at[both, there], zb.at[z], to_z(k)))
        zb[z] = total[both, b_rows]
        for j in range(2):
            ya[j, y] = total[j, a_rows]

        arrive(to_zb)
        yb[y] = add_all([zb[k].astype(F32) for k in range(NZ)]).astype(BF16)
        to_yb = [send(yb.at[y], yb.at[y], to_y(k)) for k in ORDER_8]
        to_za = []
        for j in range(2):
            arrive(to_ya[j])
            za[j, z] = add_all([ya[j, k].astype(F32) for k in range(NY)]).astype(BF16)
            to_za.append([send(za.at[j, z], za.at[j, z], to_z(k)) for k in ORDER_4])
            if j == 0:
                extra = ride(2, extra)

        ride(3, extra)
        from_ya = []

        def gather_a(j):
            arrive(to_za[j])
            mine = full.at[core, j, a_rows]
            mine[...] = finish(j, add_all([za[j, k].astype(F32) for k in range(NZ)])).astype(BF16)
            from_ya.append([send(mine, mine, to_y(k)) for k in ORDER_8])

        gather_a(0)
        arrive(to_yb)
        mine = full.at[core, both, b_rows]
        mine[...] = finish(2, add_all([yb[k].astype(F32) for k in range(NY)])).astype(BF16)
        from_zb = [send(mine, mine, to_z(k)) for k in ORDER_4]
        gather_a(1)
        ride(4, None)
        across = []
        for j in range(2):
            arrive(from_ya[j])
            mine = full.at[core, j, upper]
            across.append([send(mine, mine, partner)])
            yield core, j, across[j]
        for j in range(2):
            arrive(across[j])
        yield 1 - core, 0, None
        arrive(from_zb)
        mine = full.at[core, both, lower]
        across = [send(mine, mine, partner)]
        yield core, 2, None
        arrive(across)
        yield 1 - core, 2, None

    norms = []

    def damped(part, value):
        if part < 2:
            lane = pl.multiple_of(core * half + part * LANES, LANES)
            value = value + DAMPING * w_ref[a_rows, pl.ds(lane, LANES)].astype(F32)
            grad_a[part] = value
            norms.append(total_of(value * value) / NZ)
        else:
            lane = pl.multiple_of(core * half, half)
            weight = w_ref[b_rows, pl.ds(lane, half)].astype(F32)
            value = value + DAMPING * jnp.stack([weight[:, :LANES], weight[:, LANES:]])
            grad_b[...] = value
            norms.append(total_of(value[0] * value[0] + value[1] * value[1]) / NY)
        return value

    arrivals = []
    for side, part, _ in sum_rows(
            err, grad, damped, g_sum, g_ya, g_za, g_zb, g_yb, lambda *_: None):
        here = slice(0, top) if part < 2 else slice(top, depth)
        if part == 0 and _ is not None:
            continue
        mat = jnp.concatenate([grad[side, 0, here], grad[side, 1, here]], axis=1)
        value = jnp.dot(x_ref[:, here], mat, preferred_element_type=F32)
        if part < 2:
            pacc[side] = value
        else:
            proj[side] = (pacc[side] + value).astype(BF16).reshape(proj.shape[1:])
            arrivals += [send(proj.at[side, lax.rem(feat + k, NF)], got_p.at[side, feat], to_feat(k)) for k in ORDER_8]
    norm = add_all(norms)
    for side in range(2):
        got_p[side, feat] = proj[side, feat]
    arrive(arrivals)
    quarters = [(side, j) for side in range(2) for j in range(2)]
    pj = [add_all([got_p[side, k, :, j * LANES:(j + 1) * LANES].astype(F32) for k in range(NF)]) for side, j in quarters]
    ps = [probs[side, :, j * LANES:(j + 1) * LANES] for side, j in quarters]
    pp = [a * b for a, b in zip(ps, pj)]
    inner = jnp.sum(add_all(pp), axis=1, keepdims=True)
    scale = count / total_samples
    weighted = [((a - b * inner) * scale).astype(BF16) for a, b in zip(pp, ps)]
    for (side, j), value in zip(quarters, weighted):
        wgt_out[lax.rem(core + side, 2), :, j * LANES:(j + 1) * LANES] = value
    copies = to_chips(wgt_out, wgt)
    curv = total_of(add_all([a.astype(F32) * b for a, b in zip(weighted, pj)]))
    upper_half = lax.broadcasted_iota(jnp.int32, (8, LANES), 0) < 4
    sc_own[...] = jnp.where(upper_half, norm, curv)
    scalars = [send(sc_own, sc_f.at[1, feat], partner)]
    for k in ORDER_8:
        scalars.append(send(sc_own, sc_f.at[0, feat], to_feat(k)))
        scalars.append(send(sc_own, sc_f.at[1, feat], to_other(k)))
    sc_f[0, feat] = sc_own[...]
    arrive(copies)

    alpha = []

    def ride(stage, copies):
        if stage == 1:
            arrive(scalars)
            both_cores = [add_all([sc_f[lax.rem(core + one, 2), k] for k in range(NF)]) for one in range(2)]
            sc_y[y] = both_cores[0] + both_cores[1]
            return [send(sc_y.at[y], sc_y.at[y], to_y(k)) for k in ORDER_8]
        if copies:
            arrive(copies)
        if stage == 2:
            sc_z[z] = add_all([sc_y[k] for k in range(NY)])
            return [send(sc_z.at[z], sc_z.at[z], to_z(k)) for k in ORDER_4]
        if stage == 3:
            sums = add_all([sc_z[k] for k in range(NZ)])
            alpha.append(sums[0:1, 0:1] / (sums[4:5, 0:1] + DAMPING * sums[0:1, 0:1]))
        else:
            for side, j in quarters:
                step_ref[side, j] = (-alpha[0] * grad[side, j].astype(F32)).astype(BF16)
                store(step_ref, step_out, side, j, pl.ds(0, depth))
        return None

    def residual(part, value):
        g = grad_a[part] if part < 2 else grad_b[...]
        return -g + alpha[0] * (value + DAMPING * g)

    stored = []

    def store(src, dst, side, j, here):
        lanes = pl.ds(pl.multiple_of((2 * side + j) * LANES, LANES), LANES)
        copy = pltpu.make_async_copy(src.at[side, j, here], dst.at[here, lanes], stores.at[len(stored)])
        copy.start()
        stored.append(copy)

    for side, part, _ in sum_rows(
            wgt, resid, residual, i_sum, i_ya, i_za, i_zb, i_yb, ride):
        if part == 2:
            for j in range(2):
                store(resid, resid_out, side, j, lower)
        elif _ is not None:
            store(resid, resid_out, side, part, upper)
        else:
            for j in range(2):
                store(resid, resid_out, side, j, upper)
    for copy in stored:
        copy.wait()
    for copy in pending:
        copy.wait_send()


def write(step_ref, resid_ref, step_out, resid_out, held, ins, outs):
    depth = step_ref.shape[0]
    loads, stores = [], []
    for n, (src, dst) in enumerate(((step_ref, step_out), (resid_ref, resid_out))):
        for part in range(4):
            some = pl.ds(part * (depth // 4), depth // 4)
            index = len(loads)
            loads.append(pltpu.make_async_copy(src.at[some], held.at[n, some], ins.at[index]))
            stores.append(pltpu.make_async_copy(held.at[n, some], dst.at[some], outs.at[index]))
    for copy in loads:
        copy.start()
    for there, back in zip(loads, stores):
        there.wait()
        back.start()
    for copy in stores:
        copy.wait()


def body(features, labels, probe_weight, sampled):
    height, depth = features.shape
    classes = probe_weight.shape[1]
    half = classes // 2
    own = height // NF
    top = depth * 2 // 3
    pa, pb = top // NY, (depth - top) // NZ
    hbm = pl.BlockSpec(memory_space=pltpu.HBM)
    out = jax.ShapeDtypeStruct((depth, classes), BF16)
    labels = labels.reshape(1, height)
    sampled = sampled.reshape(1, sampled.shape[0])

    def chain():
        return [
            pltpu.VMEM((2, depth, LANES), BF16),
            pltpu.VMEM((2, NY, pa, LANES), BF16),
            pltpu.VMEM((2, NZ, pa, LANES), BF16),
            pltpu.VMEM((NZ, 2, pb, LANES), BF16),
            pltpu.VMEM((NY, 2, pb, LANES), BF16),
        ]

    step, resid = pl.pallas_call(
        kernel,
        out_shape=(out, out),
        in_specs=[hbm] * 4,
        out_specs=(hbm, hbm),
        scratch_shapes=[
            pltpu.VMEM((2, 2, depth, LANES), BF16),
            pltpu.VMEM((2, 2, depth, LANES), BF16),
            pltpu.VMEM(features.shape, BF16),
            pltpu.VMEM(labels.shape, jnp.int32),
            pltpu.VMEM(probe_weight.shape, BF16),
            pltpu.VMEM(sampled.shape, jnp.int32),
            pltpu.VMEM(features.shape, BF16),
            pltpu.VMEM((depth, 2 * height), BF16),
            pltpu.VMEM((NF, own // 16 * 5, 16, LANES), jnp.int16),
            pltpu.VMEM((NF, own // 16 * 5, 16, LANES), jnp.int16),
            pltpu.VMEM((2, own, half), BF16),
            pltpu.VMEM((2, NF, own, half), BF16),
            pltpu.VMEM((2, own, half), F32),
            *chain(),
            pltpu.VMEM((2, pa, LANES), F32),
            pltpu.VMEM((2, pb, LANES), F32),
            pltpu.VMEM((2, 2, depth, LANES), BF16),
            pltpu.VMEM((2, height, half), F32),
            pltpu.VMEM((2, NF, own, half), BF16),
            pltpu.VMEM((2, NF, own, half), BF16),
            pltpu.VMEM((2, own, half), BF16),
            pltpu.VMEM((2, NF, own, half), BF16),
            *chain(),
            pltpu.VMEM((8, LANES), F32),
            pltpu.VMEM((2, NF, 8, LANES), F32),
            pltpu.VMEM((NY, 8, LANES), F32),
            pltpu.VMEM((NZ, 8, LANES), F32),
            pltpu.SemaphoreType.DMA((4,)),
            pltpu.SemaphoreType.DMA((16,)),
            pltpu.SemaphoreType.DMA((208,)),
            pltpu.SemaphoreType.DMA((208,)),
        ],
        compiler_params=pltpu.CompilerParams(
            collective_id=0, has_side_effects=True, vmem_limit_bytes=VMEM_BYTES
        ),
    )(features, labels, probe_weight, sampled)
    return pl.pallas_call(
        write,
        out_shape=(out, out),
        in_specs=[hbm] * 2,
        out_specs=(hbm, hbm),
        scratch_shapes=[
            pltpu.VMEM((2, depth, classes), BF16),
            pltpu.SemaphoreType.DMA((16,)),
            pltpu.SemaphoreType.DMA((16,)),
        ],
        compiler_params=pltpu.CompilerParams(vmem_limit_bytes=VMEM_BYTES),
    )(step, resid)


def solution(mesh):
    in_specs = (P("rows", "feat"), P("rows"), P("feat", None), P("rows"))
    out_specs = (P("feat", None), P("feat", None))
    return jax.shard_map(body, mesh=mesh, in_specs=in_specs, out_specs=out_specs, check_vma=False)
```

```python
import functools

import jax
import jax.numpy as jnp
from jax import lax
from jax.experimental import pallas as pl
from jax.experimental.pallas import tpu as pltpu
from jax.sharding import PartitionSpec as P

MESH = pl.DeviceIdType.MESH
DAMPING = 0.01
F32, BF16 = jnp.float32, jnp.bfloat16
NF, NZ, NY, LANES = 8, 4, 8, 128
FULL = 15.0 - 1.0 / 256.0
VMEM_BYTES = 56 * 1024 * 1024
ORDER_8, ORDER_4 = (4, 3, 5, 2, 6, 1, 7), (2, 1, 3)


def add_all(values):
    return functools.reduce(jnp.add, values)


def total_of(value):
    return jnp.sum(jnp.sum(value, axis=1, keepdims=True), axis=0, keepdims=True)


def kernel(x_hbm, lab_hbm, w_hbm, smp_hbm, step_out, resid_out, step_ref, resid, x_ref, lab_ref, w_ref, smp_ref, x_other, xt, part, got_l, err_out, err, probs,
           g_sum, g_ya, g_za, g_zb, g_yb, grad_a, grad_b, grad, pacc, proj, got_p,
           wgt_out, wgt, i_sum, i_ya, i_za, i_zb, i_yb,
           sc_own, sc_f, sc_y, sc_z, loads, stores, sends, recvs):
    rows = lax.axis_index("rows")
    feat = lax.axis_index("feat")
    core = lax.rem(rows, 2)
    y = lax.rem(rows // 2, NY)
    z = rows // (2 * NY)
    height, depth = x_ref.shape
    own = height // NF
    half = w_ref.shape[1] // 2
    tiles = own // 16 * 4
    top = depth * 2 // 3
    pa, pb = top // NY, (depth - top) // NZ
    total_rows = height * NF * 8
    total_samples = smp_ref.shape[1] * NF * 8

    loaded = [pltpu.make_async_copy(src, dst, loads.at[i]) for i, (src, dst) in enumerate(
        ((x_hbm, x_ref), (w_hbm, w_ref), (lab_hbm, lab_ref), (smp_hbm, smp_ref)))]
    for copy in loaded:
        copy.start()

    def to_feat(k):
        return {"rows": rows, "feat": lax.rem(feat + k, NF)}

    def to_y(k):
        return {"rows": (z * NY + lax.rem(y + k, NY)) * 2 + core, "feat": feat}

    def to_z(k):
        return {"rows": (lax.rem(z + k, NZ) * NY + y) * 2 + core, "feat": feat}

    partner = {"rows": rows + 1 - 2 * core, "feat": feat}

    def to_other(k):
        return {"rows": rows + 1 - 2 * core, "feat": lax.rem(feat + k, NF)}

    pending = []

    def send(src, dst, where):
        index = len(pending)
        copy = pltpu.make_async_remote_copy(
            src_ref=src, dst_ref=dst, send_sem=sends.at[index], recv_sem=recvs.at[index], device_id=where,
            device_id_type=MESH,
        )
        copy.start()
        pending.append(copy)
        return copy

    def arrive(copies):
        for copy in copies:
            copy.wait_recv()

    barrier = pltpu.get_barrier_semaphore()
    peers = [to_y(4), to_z(2)] + [to_y(k) for k in (3, 5)] + [to_feat(k) for k in (3, 5, 4)]
    peers += [to_other(k) for k in ORDER_8] + [to_z(1), to_z(3), to_y(2), to_y(6)] + [to_feat(k) for k in (2, 6, 1, 7)] + [to_y(1), to_y(7), partner]
    for where in peers:
        pl.semaphore_signal(barrier, inc=1, device_id=where, device_id_type=MESH)

    loaded[0].wait()
    loaded[1].wait()
    value = jnp.dot(x_ref[...], w_ref[...], preferred_element_type=F32)
    largest = jnp.maximum(jnp.max(jnp.abs(value), axis=1, keepdims=True), 1e-30)
    power = jnp.ceil(jnp.log2(largest) * 16.0)
    codes = jnp.round(value * jnp.exp2(FULL - power / 16.0)).astype(jnp.int32).astype(jnp.int16)
    powers = jnp.broadcast_to(power, (height, LANES)).astype(jnp.int32).astype(jnp.int16)
    for i in range(NF):
        for r in range(own // 16):
            for c in range(4):
                part[i, 4 * r + c] = codes[i * own + 16 * r:i * own + 16 * (r + 1), c * LANES:(c + 1) * LANES]
            part[i, tiles + r] = powers[i * own + 16 * r:i * own + 16 * (r + 1)]
    pl.semaphore_wait(barrier, len(peers))
    copies = [send(part.at[lax.rem(feat + k, NF)], got_l.at[feat], to_feat(k)) for k in ORDER_8]
    copy_x = send(x_ref, x_other, partner)
    xt[:, :height] = x_ref[...].T
    loaded[2].wait()
    loaded[3].wait()
    row_id = feat * own + lax.broadcasted_iota(jnp.int32, (own, height), 0)
    here = row_id == lax.broadcasted_iota(jnp.int32, (own, height), 1)
    label = jnp.sum(jnp.where(here, lab_ref[...], 0), axis=1, keepdims=True)
    sample_id = feat * own + lax.broadcasted_iota(jnp.int32, (own, smp_ref.shape[1]), 0)
    count = jnp.sum(jnp.where(sample_id == smp_ref[...], 1.0, 0.0), axis=1, keepdims=True)
    got_l[feat] = part[feat]
    arrive([copy_x])
    xt[:, height:] = x_other[...].T
    arrive(copies)
    pieces = range(own // 16)
    units = [[jnp.exp2(got_l[k, tiles + r].astype(jnp.int32).astype(F32) / 16.0 - FULL) for r in pieces] for k in range(NF)]
    blocks = []
    for c in range(4):
        blocks.append(jnp.concatenate([
            add_all([got_l[k, 4 * r + c].astype(jnp.int32).astype(F32) * units[k][r] for k in range(NF)])
            for r in pieces], axis=0))
    logits = [jnp.concatenate(blocks[2 * side:2 * side + 2], axis=1) for side in range(2)]
    highest = jnp.max(jnp.maximum(*logits), axis=1, keepdims=True)
    expo = [jnp.exp(value - highest) for value in logits]
    bottom = jnp.sum(expo[0] + expo[1], axis=1, keepdims=True)
    for side in range(2):
        p = expo[side] / bottom
        probs[side] = p
        class_id = side * half + lax.broadcasted_iota(jnp.int32, p.shape, 1)
        err_out[lax.rem(core + side, 2)] = ((p - jnp.where(label == class_id, 1.0, 0.0)) / total_rows).astype(BF16)

    def to_chips(out, into):
        copies = []
        for k in ORDER_8:
            copies.append(send(out.at[0], into.at[0, feat], to_feat(k)))
            copies.append(send(out.at[1], into.at[1, feat], to_other(k)))
        copies.append(send(out.at[1], into.at[1, feat], partner))
        into[0, feat] = out[0]
        return copies

    arrive(to_chips(err_out, err))

    def rows_at(start, size):
        return pl.ds(pl.multiple_of(start, size), size)

    a_rows = rows_at(y * pa, pa)
    b_rows = rows_at(top + z * pb, pb)
    both, upper, lower = pl.ds(0, 2), pl.ds(0, top), pl.ds(top, depth - top)

    def sum_rows(mat, full, finish, total, ya, za, zb, yb, ride):
        def times(start, stop):
            value = jnp.dot(xt[start:stop], mat[...].reshape(2 * height, half), preferred_element_type=F32).astype(BF16)
            for j in range(2):
                total[j, start:stop] = value[:, j * LANES:(j + 1) * LANES]

        times(0, top)
        to_ya = []
        for j in range(2):
            to_ya.append([send(total.at[j, rows_at(lax.rem(y + k, NY) * pa, pa)], ya.at[j, y], to_y(k)) for k in ORDER_8])
            if j == 0:
                extra = ride(1, None)
        times(top, depth)
        to_zb = []
        for k in ORDER_4:
            there = rows_at(top + lax.rem(z + k, NZ) * pb, pb)
            to_zb.append(send(total.at[both, there], zb.at[z], to_z(k)))
        zb[z] = total[both, b_rows]
        for j in range(2):
            ya[j, y] = total[j, a_rows]

        arrive(to_zb)
        yb[y] = add_all([zb[k].astype(F32) for k in range(NZ)]).astype(BF16)
        to_yb = [send(yb.at[y], yb.at[y], to_y(k)) for k in ORDER_8]
        to_za = []
        for j in range(2):
            arrive(to_ya[j])
            za[j, z] = add_all([ya[j, k].astype(F32) for k in range(NY)]).astype(BF16)
            to_za.append([send(za.at[j, z], za.at[j, z], to_z(k)) for k in ORDER_4])
            if j == 0:
                extra = ride(2, extra)

        ride(3, extra)
        from_ya = []

        def gather_a(j):
            arrive(to_za[j])
            mine = full.at[core, j, a_rows]
            mine[...] = finish(j, add_all([za[j, k].astype(F32) for k in range(NZ)])).astype(BF16)
            from_ya.append([send(mine, mine, to_y(k)) for k in ORDER_8])

        gather_a(0)
        arrive(to_yb)
        mine = full.at[core, both, b_rows]
        mine[...] = finish(2, add_all([yb[k].astype(F32) for k in range(NY)])).astype(BF16)
        from_zb = [send(mine, mine, to_z(k)) for k in ORDER_4]
        gather_a(1)
        ride(4, None)
        across = []
        for j in range(2):
            arrive(from_ya[j])
            mine = full.at[core, j, upper]
            across.append([send(mine, mine, partner)])
            yield core, j, across[j]
        for j in range(2):
            arrive(across[j])
        yield 1 - core, 0, None
        arrive(from_zb)
        mine = full.at[core, both, lower]
        across = [send(mine, mine, partner)]
        yield core, 2, None
        arrive(across)
        yield 1 - core, 2, None

    norms = []

    def damped(part, value):
        if part < 2:
            lane = pl.multiple_of(core * half + part * LANES, LANES)
            value = value + DAMPING * w_ref[a_rows, pl.ds(lane, LANES)].astype(F32)
            grad_a[part] = value
            norms.append(total_of(value * value) / NZ)
        else:
            lane = pl.multiple_of(core * half, half)
            weight = w_ref[b_rows, pl.ds(lane, half)].astype(F32)
            value = value + DAMPING * jnp.stack([weight[:, :LANES], weight[:, LANES:]])
            grad_b[...] = value
            norms.append(total_of(value[0] * value[0] + value[1] * value[1]) / NY)
        return value

    arrivals = []
    for side, part, _ in sum_rows(
            err, grad, damped, g_sum, g_ya, g_za, g_zb, g_yb, lambda *_: None):
        here = slice(0, top) if part < 2 else slice(top, depth)
        if part == 0 and _ is not None:
            continue
        mat = jnp.concatenate([grad[side, 0, here], grad[side, 1, here]], axis=1)
        value = jnp.dot(x_ref[:, here], mat, preferred_element_type=F32)
        if part < 2:
            pacc[side] = value
        else:
            proj[side] = (pacc[side] + value).astype(BF16).reshape(proj.shape[1:])
            arrivals += [send(proj.at[side, lax.rem(feat + k, NF)], got_p.at[side, feat], to_feat(k)) for k in ORDER_8]
    norm = add_all(norms)
    for side in range(2):
        got_p[side, feat] = proj[side, feat]
    arrive(arrivals)
    quarters = [(side, j) for side in range(2) for j in range(2)]
    pj = [add_all([got_p[side, k, :, j * LANES:(j + 1) * LANES].astype(F32) for k in range(NF)]) for side, j in quarters]
    ps = [probs[side, :, j * LANES:(j + 1) * LANES] for side, j in quarters]
    pp = [a * b for a, b in zip(ps, pj)]
    inner = jnp.sum(add_all(pp), axis=1, keepdims=True)
    scale = count / total_samples
    weighted = [((a - b * inner) * scale).astype(BF16) for a, b in zip(pp, ps)]
    for (side, j), value in zip(quarters, weighted):
        wgt_out[lax.rem(core + side, 2), :, j * LANES:(j + 1) * LANES] = value
    copies = to_chips(wgt_out, wgt)
    curv = total_of(add_all([a.astype(F32) * b for a, b in zip(weighted, pj)]))
    upper_half = lax.broadcasted_iota(jnp.int32, (8, LANES), 0) < 4
    sc_own[...] = jnp.where(upper_half, norm, curv)
    scalars = [send(sc_own, sc_f.at[1, feat], partner)]
    for k in ORDER_8:
        scalars.append(send(sc_own, sc_f.at[0, feat], to_feat(k)))
        scalars.append(send(sc_own, sc_f.at[1, feat], to_other(k)))
    sc_f[0, feat] = sc_own[...]
    arrive(copies)

    alpha = []

    def ride(stage, copies):
        if stage == 1:
            arrive(scalars)
            both_cores = [add_all([sc_f[lax.rem(core + one, 2), k] for k in range(NF)]) for one in range(2)]
            sc_y[y] = both_cores[0] + both_cores[1]
            return [send(sc_y.at[y], sc_y.at[y], to_y(k)) for k in ORDER_8]
        if copies:
            arrive(copies)
        if stage == 2:
            sc_z[z] = add_all([sc_y[k] for k in range(NY)])
            return [send(sc_z.at[z], sc_z.at[z], to_z(k)) for k in ORDER_4]
        if stage == 3:
            sums = add_all([sc_z[k] for k in range(NZ)])
            alpha.append(sums[0:1, 0:1] / (sums[4:5, 0:1] + DAMPING * sums[0:1, 0:1]))
        else:
            for side, j in quarters:
                step_ref[side, j] = (-alpha[0] * grad[side, j].astype(F32)).astype(BF16)
                store(step_ref, step_out, side, j, pl.ds(0, depth))
        return None

    def residual(part, value):
        g = grad_a[part] if part < 2 else grad_b[...]
        return -g + alpha[0] * (value + DAMPING * g)

    stored = []

    def store(src, dst, side, j, here):
        lanes = pl.ds(pl.multiple_of((2 * side + j) * LANES, LANES), LANES)
        copy = pltpu.make_async_copy(src.at[side, j, here], dst.at[here, lanes], stores.at[len(stored)])
        copy.start()
        stored.append(copy)

    for side, part, _ in sum_rows(
            wgt, resid, residual, i_sum, i_ya, i_za, i_zb, i_yb, ride):
        if part == 2:
            for j in range(2):
                store(resid, resid_out, side, j, lower)
        elif _ is not None:
            store(resid, resid_out, side, part, upper)
        else:
            for j in range(2):
                store(resid, resid_out, side, j, upper)
    for copy in stored:
        copy.wait()
    for copy in pending:
        copy.wait_send()


def write(step_ref, resid_ref, step_out, resid_out, held, ins, outs):
    depth = step_ref.shape[0]
    loads, stores = [], []
    for n, (src, dst) in enumerate(((step_ref, step_out), (resid_ref, resid_out))):
        for part in range(4):
            some = pl.ds(part * (depth // 4), depth // 4)
            index = len(loads)
            loads.append(pltpu.make_async_copy(src.at[some], held.at[n, some], ins.at[index]))
            stores.append(pltpu.make_async_copy(held.at[n, some], dst.at[some], outs.at[index]))
    for copy in loads:
        copy.start()
    for there, back in zip(loads, stores):
        there.wait()
        back.start()
    for copy in stores:
        copy.wait()


def body(features, labels, probe_weight, sampled):
    height, depth = features.shape
    classes = probe_weight.shape[1]
    half = classes // 2
    own = height // NF
    top = depth * 2 // 3
    pa, pb = top // NY, (depth - top) // NZ
    hbm = pl.BlockSpec(memory_space=pltpu.HBM)
    out = jax.ShapeDtypeStruct((depth, classes), BF16)
    labels = labels.reshape(1, height)
    sampled = sampled.reshape(1, sampled.shape[0])

    def chain():
        return [
            pltpu.VMEM((2, depth, LANES), BF16),
            pltpu.VMEM((2, NY, pa, LANES), BF16),
            pltpu.VMEM((2, NZ, pa, LANES), BF16),
            pltpu.VMEM((NZ, 2, pb, LANES), BF16),
            pltpu.VMEM((NY, 2, pb, LANES), BF16),
        ]

    step, resid = pl.pallas_call(
        kernel,
        out_shape=(out, out),
        in_specs=[hbm] * 4,
        out_specs=(hbm, hbm),
        scratch_shapes=[
            pltpu.VMEM((2, 2, depth, LANES), BF16),
            pltpu.VMEM((2, 2, depth, LANES), BF16),
            pltpu.VMEM(features.shape, BF16),
            pltpu.VMEM(labels.shape, jnp.int32),
            pltpu.VMEM(probe_weight.shape, BF16),
            pltpu.VMEM(sampled.shape, jnp.int32),
            pltpu.VMEM(features.shape, BF16),
            pltpu.VMEM((depth, 2 * height), BF16),
            pltpu.VMEM((NF, own // 16 * 5, 16, LANES), jnp.int16),
            pltpu.VMEM((NF, own // 16 * 5, 16, LANES), jnp.int16),
            pltpu.VMEM((2, own, half), BF16),
            pltpu.VMEM((2, NF, own, half), BF16),
            pltpu.VMEM((2, own, half), F32),
            *chain(),
            pltpu.VMEM((2, pa, LANES), F32),
            pltpu.VMEM((2, pb, LANES), F32),
            pltpu.VMEM((2, 2, depth, LANES), BF16),
            pltpu.VMEM((2, height, half), F32),
            pltpu.VMEM((2, NF, own, half), BF16),
            pltpu.VMEM((2, NF, own, half), BF16),
            pltpu.VMEM((2, own, half), BF16),
            pltpu.VMEM((2, NF, own, half), BF16),
            *chain(),
            pltpu.VMEM((8, LANES), F32),
            pltpu.VMEM((2, NF, 8, LANES), F32),
            pltpu.VMEM((NY, 8, LANES), F32),
            pltpu.VMEM((NZ, 8, LANES), F32),
            pltpu.SemaphoreType.DMA((4,)),
            pltpu.SemaphoreType.DMA((16,)),
            pltpu.SemaphoreType.DMA((208,)),
            pltpu.SemaphoreType.DMA((208,)),
        ],
        compiler_params=pltpu.CompilerParams(
            collective_id=0, has_side_effects=True, vmem_limit_bytes=VMEM_BYTES
        ),
    )(features, labels, probe_weight, sampled)
    return pl.pallas_call(
        write,
        out_shape=(out, out),
        in_specs=[hbm] * 2,
        out_specs=(hbm, hbm),
        scratch_shapes=[
            pltpu.VMEM((2, depth, classes), BF16),
            pltpu.SemaphoreType.DMA((16,)),
            pltpu.SemaphoreType.DMA((16,)),
        ],
        compiler_params=pltpu.CompilerParams(vmem_limit_bytes=VMEM_BYTES),
    )(step, resid)


def solution(mesh):
    in_specs = (P("rows", "feat"), P("rows"), P("feat", None), P("rows"))
    out_specs = (P("feat", None), P("feat", None))
    return jax.shard_map(body, mesh=mesh, in_specs=in_specs, out_specs=out_specs, check_vma=False)
```
